512 devices in a mesh: dp: 8 (over x, z_hi), mp: 64 (over z_lo, y, core).
Axes of the slice: x: 4, y: 8, z: 8 (z_hi: 2, z_lo: 4; z = z_hi * 4 + z_lo), core: 2. Of those that a mesh axis runs over, the one named last changes fastest.
Arguments:
- acts: bfloat16 [2048, 28672], P('dp', 'mp'), may hold values from -6 to 6
- grads: bfloat16 [2048, 8192], P('dp', 'mp'), may hold values from -6 to 6
- basis_in: bfloat16 [3584, 28672], P('mp'), may hold values from -0.03125 to 0.03125
- basis_out: bfloat16 [512, 8192], P('mp'), may hold values from -0.0625 to 0.0625
- doc_lengths: int32 [8, 4], P('dp'), may hold values from 1 to 128, 256 in all within a row
Outputs:
- correction: float32 [512, 3584], P('dp', 'mp')
The draws below stay inside these ranges and needn't reach their ends.
Inputs may be any that keep to these rules, and one draw needn't show every extreme that they name: `doc_lengths`: each row holds 4 lengths that sum to 256; the largest of each row is exactly 128.
All inputs are finite; a program needn't handle non-finite values.
Results may differ from the reference program's by a relative error of at most 0.0019.
Values may be sent and summed in bfloat16 or wider, within the bound.
No kernel may reach another device: no remote copies, remote signals or barrier semaphores. Data moves between devices by JAX's collectives and lax.ppermute only.
A program may use at most 64 MiB of HBM per device.

```python
import math
import jax
import jax.numpy as jnp
import numpy as np
from jax import lax

DIN = 28672
DOUT = 8192
TOK_DP = 256
DOCS = 4
KA = 3584
KG = 512
TOKENS = 2048
N_DP = 8


def block_levels(key, dims, pieces, low, largest):
    def one(dim, blocks):
        steps = jax.random.uniform(jax.random.fold_in(jax.random.fold_in(key, 6), dim), (blocks,), jnp.float32, low / len(pieces), largest / len(pieces))
        return jnp.repeat(jnp.exp(steps), dims[dim] // blocks).reshape((-1,) + (1,) * (len(dims) - dim - 1))

    gain = one(*pieces[0])
    for cut in pieces[1:]:
        gain = gain * one(*cut)
    return gain


def profile(amount, total, most, skew):
    loads = [(1 << 20) // math.isqrt(standing ** skew) + 1 for standing in range(2, amount + 1)]
    spare, holding = total - most - (amount - 1), [1] * (amount - 1)
    while spare > 0:
        movable = [i for i in range(amount - 1) if holding[i] < most]
        mass, budget = sum([loads[i] for i in movable]), spare
        for i in movable:
            more = min(most - holding[i], max(1, budget * loads[i] // mass), spare)
            holding[i] = holding[i] + more
            spare = spare - more
    return np.array([most] + holding)


def uneven(own_key, count, total, most, slope):
    if count == 2:
        one = jax.random.randint(own_key, (), max(1, total - most), min(most, total - 1) + 1)
        return jnp.stack([one, total - one])
    sizes = jnp.asarray(profile(count, total, most, slope), jnp.int32)
    twos = (count - 1) // 2
    source_of, sink = sizes[1:1 + 2 * twos:2], sizes[2:2 + 2 * twos:2]
    room = jnp.minimum(source_of - 1, most - sink)
    moved = jax.random.randint(jax.random.fold_in(own_key, 1), (twos,), 0, 1 << 20) % (room + 1)
    sizes = sizes.at[1:1 + 2 * twos:2].set(source_of - moved).at[2:2 + 2 * twos:2].set(sink + moved)
    return sizes[jax.random.permutation(jax.random.fold_in(own_key, 2), count)]


def scatter_about(own_key, extent, deviation, limit, shards=(), kind=jnp.bfloat16):
    values = deviation * jax.random.normal(own_key, extent, jnp.float32)
    if shards:
        values = values * block_levels(own_key, extent, shards, -0.22, 0.18)
    return jnp.clip(values, -limit, limit).astype(kind)


def setup_inputs(seed: int = 0) -> dict:
    key_list = jax.random.split(jax.random.key(seed), 6)
    return {
        "acts": scatter_about(key_list[0], (TOKENS, DIN), 1.0, 6.0, ((0, 8), (1, 64))),
        "grads": scatter_about(key_list[1], (TOKENS, DOUT), 1.0, 6.0, ((0, 8), (1, 64))),
        "basis_in": scatter_about(key_list[2], (KA, DIN), DIN ** -0.5, 0.03125, ((0, 64),)),
        "basis_out": scatter_about(key_list[3], (KG, DOUT), DOUT ** -0.5, 0.0625, ((0, 64),)),
        "doc_lengths": jax.vmap(lambda own: uneven(own, DOCS, TOK_DP, TOK_DP // 2, 1))(jax.random.split(key_list[4], N_DP)).reshape((N_DP, DOCS)).astype(jnp.int32),
    }


def reference(acts, grads, basis_in, basis_out, doc_lengths):
    contract = (((1,), (1,)), ((), ()))
    proj_in = lax.dot_general(acts, basis_in, contract, preferred_element_type=jnp.float32).astype(jnp.bfloat16)
    proj_out = lax.dot_general(grads, basis_out, contract, preferred_element_type=jnp.float32).astype(jnp.bfloat16)
    starts = jnp.cumsum(doc_lengths, axis=1) - doc_lengths
    ends = starts + doc_lengths
    position = jnp.arange(TOK_DP, dtype=jnp.int32)
    masks = ((position[None, None, :] >= starts[:, :, None]) & (position[None, None, :] < ends[:, :, None]))
    masks = masks.astype(proj_in.dtype)

    def group_step(index, total):
        first = (index * TOK_DP).astype(jnp.int32)
        rows_in = lax.dynamic_slice_in_dim(proj_in, first, TOK_DP, 0)
        rows_out = lax.dynamic_slice_in_dim(proj_out, first, TOK_DP, 0)
        group_masks = lax.dynamic_index_in_dim(masks, index, 0, keepdims=False)
        for doc in range(DOCS):
            masked = rows_out * group_masks[doc][:, None]
            doc_grad = jnp.dot(masked.T, rows_in, preferred_element_type=jnp.float32)
            total = total + doc_grad * doc_grad
        return total

    total = lax.fori_loop(0, N_DP, group_step, jnp.zeros((KG, KA), jnp.float32))
    return total / jnp.float32(TOKENS)
```

```python
import functools

import jax
import jax.numpy as jnp
from jax import lax
from jax.experimental import pallas as pl
from jax.experimental.pallas import tpu as pltpu
from jax.sharding import Mesh, PartitionSpec as P

NX, NZH, NZL, NY, NC = 4, 2, 4, 8, 2
CHIPS = NZL * NY
BF16, F32 = jnp.bfloat16, jnp.float32
SMEM = pl.BlockSpec(memory_space=pltpu.SMEM)
VMEM = pl.BlockSpec(memory_space=pltpu.VMEM)


def from_offset(value, axis, size, offset):
    return lax.ppermute(value, axis, [((i + offset) % size, i) for i in range(size)])


def call(kernel, shapes, scratch, operands, flops):
    size = sum(a.size * a.dtype.itemsize for a in operands)
    return pl.pallas_call(
        kernel,
        out_shape=shapes,
        in_specs=[SMEM] + [VMEM] * (len(operands) - 1),
        out_specs=jax.tree.map(lambda _: VMEM, shapes),
        scratch_shapes=scratch,
        compiler_params=pltpu.CompilerParams(vmem_limit_bytes=40 << 20),
        cost_estimate=pl.CostEstimate(flops=flops, bytes_accessed=size, transcendentals=0),
    )(*operands)


def in_vmem(value):
    return pltpu.with_memory_space_constraint(value, pltpu.VMEM)


def in_hbm(shape):
    return pltpu.HBM(shape, BF16)


def project(place, packed_ref, *refs):
    own, other, (parts_ref, acts, grads, wide, low) = refs[:NX], refs[NX : 2 * NX], refs[2 * NX :]
    x, core = place[0], place[2]
    fin = acts.shape[0] // NC
    fout = grads.shape[1]
    tokens, height = acts.shape[1], CHIPS * 16
    for pieces, which in ((own, core), (other, 1 - core)):
        for s in range(NX):
            cols = slice(s * 256, (s + 1) * 256)
            acts[pl.ds(pl.multiple_of(which * fin, 16), fin), cols] = pieces[s][:fin, :]
            grads[which, :, cols] = pieces[s][fin:, :]
    left = packed_ref[:, :, : NC * fin].reshape(height, NC * fin)

    def columns(n, carry):
        cols = pl.ds(pl.multiple_of(n * 256, 256), 256)
        part = jnp.dot(left, acts[:, cols], preferred_element_type=F32)
        for h in range(2):
            wide[pl.ds(pl.multiple_of((n * 2 + h) * height, height), height), :] = part[:, h * 128 : (h + 1) * 128]
        return carry

    lax.fori_loop(0, tokens // 256, columns, 0)
    rows = packed_ref[pl.ds(x * 8, 8), :, NC * fin :].astype(F32).reshape(8, NC, 8, fout)
    part = jnp.zeros((64, tokens), F32)
    for c in range(NC):
        part += jnp.dot(rows[:, c].reshape(64, fout).astype(BF16), grads[c], preferred_element_type=F32)
    rest = part - part.astype(BF16).astype(F32)
    for half in range(2):
        for t in range(8):
            block = slice(half * 32, half * 32 + 32), slice(t * 128, (t + 1) * 128)
            wide[pl.ds(t * height + 14 + half, CHIPS, stride=16), :] = part[block]
            low[pl.ds(half * 8 + t, CHIPS, stride=16), :] = rest[block]
    for t in range(8):
        parts_ref[:, :, t * 128 : (t + 1) * 128] = wide[t * height : (t + 1) * height].astype(BF16).reshape(CHIPS, 16, 128)
    parts_ref[:, :, tokens:] = low[...].astype(BF16).reshape(CHIPS, 16, 128)


def add_up(place, lens_ref, parts_ref, in_ref, out_ref, wide, narrow):
    x = place[0]
    tokens = wide.shape[1]
    total = parts_ref[0].astype(F32)
    for i in range(1, CHIPS):
        total = total + parts_ref[i].astype(F32)
    for s in range(NX):
        source = lax.rem(x + s, NX)
        wide[:, pl.ds(pl.multiple_of(source * 256, 256), 256)] = total[:, s * 256 : (s + 1) * 256]
        for half in range(2):
            for h in range(2):
                col, row = s * 2 + h, half * 8 + s * 2 + h
                value = total[14 + half : 15 + half, col * 128 : (col + 1) * 128] + total[row : row + 1, tokens:]
                narrow[pl.ds(half * 8 + source * 2 + h, 1), :] = value
    wide[14:15, :128] = lens_ref[...]
    in_ref[...] = wide[...].astype(BF16)
    out_ref[...] = jnp.broadcast_to(narrow[...].astype(BF16)[None], out_ref.shape)


def documents(which, place, out_ref, piece0, piece1, piece2, piece3, total_ref, rows_in, rows_out):
    x, zh = place[0], place[1]
    block = lax.rem(zh + which, NZH)
    for s, ref in enumerate((piece0, piece1, piece2, piece3)):
        rows_in[lax.rem(x + s, NX)] = ref[...]
    rows_out[...] = out_ref[...].astype(F32).reshape(64 * 16, 128)
    position = lax.broadcasted_iota(jnp.int32, (1, 256), 1).astype(F32)
    total = jnp.zeros((NX * 16, 64), F32)
    for g in range(NX):
        left = rows_in[:, :, g * 256 : (g + 1) * 256].astype(F32).reshape(NX * 16, 256)
        lens = rows_in[g, :, :128].astype(F32)[14:15, :4]
        right = []
        for h in range(2):
            cut = [
                rows_out[pl.ds((zl * 16 + core) * 16 + block * 8 + g * 2 + h, NY, stride=32), :]
                for zl in range(NZL)
                for core in range(NC)
            ]
            right.append(jnp.concatenate(cut, axis=0))
        right = jnp.concatenate(right, axis=1).astype(BF16)
        masked, start = [], jnp.zeros((1, 1), F32)
        for d in range(4):
            end = start + lens[:, d : d + 1]
            inside = (position >= start) & (position < end)
            masked.append(jnp.where(inside, left, 0.0).astype(BF16))
            start = end
        product = lax.dot_general(
            jnp.concatenate(masked, axis=0), right, (((1,), (1,)), ((), ())), preferred_element_type=F32
        )
        for d in range(4):
            one = product[d * 64 : (d + 1) * 64]
            total = total + one * one
    total = total * (1.0 / 2048.0)
    for i in range(NX):
        total_ref[i * 14 : (i + 1) * 14, :] = total[i * 16 : i * 16 + 14]


def body(acts, grads, basis_in, basis_out, doc_lengths):
    x, zh, core = lax.axis_index("x"), lax.axis_index("zh"), lax.axis_index("core")
    place = jnp.stack([x, zh, core]).astype(jnp.int32)
    tok, fin = acts.shape
    fout = grads.shape[1]
    rows = basis_in.shape[0] // NX
    tokens = NX * tok

    mine = lax.dynamic_slice_in_dim(basis_in, x * rows, rows, 0)
    mine = jnp.pad(mine, ((0, 16 - rows), (0, 0))).reshape(16, CHIPS, NC * fin).swapaxes(0, 1)
    mine_out = basis_out.reshape(8, CHIPS, NC, fout).transpose(1, 2, 0, 3).reshape(CHIPS, 16, fout)
    packed = jnp.concatenate([mine, mine_out], axis=2)
    packed, acts, grads = lax.optimization_barrier((packed, acts, grads))
    packed = lax.all_to_all(packed, ("zl", "y"), split_axis=0, concat_axis=0, tiled=True)

    payload = jnp.concatenate([acts.T, grads.T], axis=0)
    own = [payload] + [from_offset(payload, "x", NX, s) for s in range(1, NX)]
    other = [from_offset(v, "core", NC, 1) for v in own]

    parts = call(
        project,
        in_hbm((CHIPS, 16, tokens + 128)),
        [
            pltpu.VMEM((NC * fin, tokens), BF16),
            pltpu.VMEM((NC, fout, tokens), BF16),
            pltpu.VMEM((8 * CHIPS * 16, 128), F32),
            pltpu.VMEM((CHIPS * 16, 128), F32),
        ],
        (place, *map(in_vmem, (packed, *own, *other))),
        2 * 512 * 1024 * 1024,
    )
    parts = lax.all_to_all(parts, ("zl", "y"), split_axis=0, concat_axis=0, tiled=True)
    lens = jnp.pad(doc_lengths.astype(F32), ((0, 0), (0, 124)))
    proj_in, proj_out = call(
        add_up,
        (jax.ShapeDtypeStruct((16, tokens), BF16), in_hbm((64, 16, 128))),
        [pltpu.VMEM((16, tokens), F32), pltpu.VMEM((16, 128), F32)],
        (place, lens, in_vmem(parts)),
        32 * 16 * 1152,
    )

    proj_out = lax.all_to_all(proj_out, ("zl", "y", "core"), split_axis=0, concat_axis=0, tiled=True)
    pieces = [proj_in] + [from_offset(proj_in, "x", NX, s) for s in range(1, NX)]
    operands = (place, *map(in_vmem, (proj_out, *pieces)))
    totals = [
        call(
            functools.partial(documents, which),
            jax.ShapeDtypeStruct((NX * rows, 64), F32),
            [pltpu.VMEM((NX, 16, tokens), BF16), pltpu.VMEM((64 * 16, 128), F32)],
            operands,
            2 * 4 * 256 * 256 * 64,
        )
        for which in range(NZH)
    ]
    return (totals[0] + from_offset(totals[1], "zh", NZH, 1)).T


def solution(mesh):
    fine = Mesh(mesh.devices.reshape(NX, NZH, NZL, NY, NC), ("x", "zh", "zl", "y", "core"))
    dp, mp = ("x", "zh"), ("zl", "y", "core")
    in_specs = (P(dp, mp), P(dp, mp), P(mp, None), P(mp, None), P(dp, None))
    return jax.shard_map(body, mesh=fine, in_specs=in_specs, out_specs=P(dp, mp), check_vma=False)
```

```python
import functools

import jax
import jax.numpy as jnp
from jax import lax
from jax.experimental import pallas as pl
from jax.experimental.pallas import tpu as pltpu
from jax.sharding import Mesh, PartitionSpec as P

NX, NZH, NZL, NY, NC = 4, 2, 4, 8, 2
CHIPS = NZL * NY
BF16, F32 = jnp.bfloat16, jnp.float32
SMEM = pl.BlockSpec(memory_space=pltpu.SMEM)
VMEM = pl.BlockSpec(memory_space=pltpu.VMEM)
ANY = pl.BlockSpec(memory_space=pl.ANY)


def from_offset(value, axis, size, offset):
    return lax.ppermute(value, axis, [((i + offset) % size, i) for i in range(size)])


def call(kernel, shapes, scratch, operands, flops, space=VMEM):
    size = sum(a.size * a.dtype.itemsize for a in operands)
    return pl.pallas_call(
        kernel,
        out_shape=shapes,
        in_specs=[SMEM] + [space] * (len(operands) - 1),
        out_specs=jax.tree.map(lambda _: space, shapes),
        scratch_shapes=scratch,
        compiler_params=pltpu.CompilerParams(vmem_limit_bytes=40 << 20),
        cost_estimate=pl.CostEstimate(flops=flops, bytes_accessed=size, transcendentals=0),
    )(*operands)


def in_vmem(value):
    return pltpu.with_memory_space_constraint(value, pltpu.VMEM)


def from_hbm(value):
    return pltpu.with_memory_space_constraint(value, pltpu.HBM)


def in_hbm(shape):
    return pltpu.HBM(shape, BF16)


def pack(place, basis_ref, out_rows_ref, acts_ref, grads_ref, packed_ref, payload_ref):
    first = place[0] * 14
    row = lax.broadcasted_iota(jnp.int32, (16, 56), 0)
    pick = (lax.broadcasted_iota(jnp.int32, (16, 56), 1) == row + first) & (row < 14)
    pick = pick.astype(F32).astype(BF16)
    width = basis_ref.shape[1] // packed_ref.shape[0]
    fout = grads_ref.shape[1]
    for c in range(packed_ref.shape[0]):
        rows = jnp.dot(pick, basis_ref[:, c * width : (c + 1) * width], preferred_element_type=F32)
        packed_ref[c, :, :width] = rows.astype(BF16)
        out = out_rows_ref[:, c * NC * fout : (c + 1) * NC * fout].astype(F32)
        packed_ref[c, :, width:] = jnp.concatenate([out[:, :fout], out[:, fout:]], axis=0).astype(BF16)

    @pl.when(pl.program_id(0) == 0)
    def _():
        fin = acts_ref.shape[0]
        payload_ref[:fin, :] = acts_ref[...]
        payload_ref[fin:, :] = grads_ref[...].astype(F32).T.astype(BF16)


def project(place, packed_ref, *refs):
    own, other, parts_ref = refs[:NX], refs[NX : 2 * NX], refs[2 * NX]
    packed, acts, grads, wide, low, *outs, in_sems, out_sems = refs[2 * NX + 1 :]
    x, core = place[0], place[2]
    fin = acts.shape[0] // NC
    fout = grads.shape[1]
    tokens, height = acts.shape[1], CHIPS * 16
    first = pltpu.make_async_copy(packed_ref, packed, in_sems.at[16])
    first.start()
    copies = []
    for s in range(NX):
        cols = pl.ds(s * 256, 256)
        for k, (pieces, which) in enumerate(((own, core), (other, 1 - core))):
            rows = pl.ds(pl.multiple_of(which * fin, 16), fin)
            copies.append(
                [
                    pltpu.make_async_copy(pieces[s].at[pl.ds(0, fin)], acts.at[rows, cols], in_sems.at[s * 4 + k * 2]),
                    pltpu.make_async_copy(
                        pieces[s].at[pl.ds(fin, fout)], grads.at[which, :, cols], in_sems.at[s * 4 + k * 2 + 1]
                    ),
                ]
            )
            for copy in copies[-1]:
                copy.start()
    first.wait()
    left = packed[:, :, : NC * fin].reshape(height, NC * fin)
    rows_out = packed[pl.ds(x * 8, 8), :, NC * fin :].astype(F32).reshape(8, NC, 8, fout)
    rows_out = [rows_out[:, c].reshape(64, fout).astype(BF16) for c in range(NC)]
    results = []
    for s in range(NX):
        for copy in copies[2 * s] + copies[2 * s + 1]:
            copy.wait()
        cols = slice(s * 256, (s + 1) * 256)
        part = jnp.dot(left, acts[:, cols], preferred_element_type=F32)
        out = jnp.zeros((64, 256), F32)
        for c in range(NC):
            out += jnp.dot(rows_out[c], grads[c, :, cols], preferred_element_type=F32)
        rest = out - out.astype(BF16).astype(F32)
        for h in range(2):
            block = slice(h * 128, (h + 1) * 128)
            wide[pl.ds(h * height, height), :] = part[:, block]
            for half in range(2):
                wide[pl.ds(h * height + 14 + half, CHIPS, stride=16), :] = out[half * 32 : half * 32 + 32, block]
                low[pl.ds(half * 8 + s * 2 + h, CHIPS, stride=16), :] = rest[half * 32 : half * 32 + 32, block]
            outs[s][:, :, block] = wide[h * height : (h + 1) * height].astype(BF16).reshape(CHIPS, 16, 128)
        results.append(pltpu.make_async_copy(outs[s], parts_ref.at[:, :, pl.ds(s * 256, 256)], out_sems.at[s]))
        results[-1].start()
    outs[NX][...] = low[...].astype(BF16).reshape(CHIPS, 16, 128)
    results.append(pltpu.make_async_copy(outs[NX], parts_ref.at[:, :, pl.ds(tokens, 128)], out_sems.at[NX]))
    results[-1].start()
    for result in results:
        result.wait()


def add_up(place, lens_ref, parts_ref, in_ref, out_ref, wide, narrow):
    x = place[0]
    tokens = wide.shape[1]
    total = parts_ref[0].astype(F32)
    for i in range(1, CHIPS):
        total = total + parts_ref[i].astype(F32)
    for s in range(NX):
        source = lax.rem(x + s, NX)
        wide[:, pl.ds(pl.multiple_of(source * 256, 256), 256)] = total[:, s * 256 : (s + 1) * 256]
        for half in range(2):
            for h in range(2):
                col, row = s * 2 + h, half * 8 + s * 2 + h
                value = total[14 + half : 15 + half, col * 128 : (col + 1) * 128] + total[row : row + 1, tokens:]
                narrow[pl.ds(half * 8 + source * 2 + h, 1), :] = value
    wide[14:15, :128] = lens_ref[...]
    in_ref[...] = wide[...].astype(BF16)
    out_ref[...] = jnp.broadcast_to(narrow[...].astype(BF16)[None], out_ref.shape)


def documents(which, place, out_ref, piece0, piece1, piece2, piece3, total_ref, rows_in, rows_out):
    x, zh = place[0], place[1]
    block = lax.rem(zh + which, NZH)
    for s, ref in enumerate((piece0, piece1, piece2, piece3)):
        rows_in[lax.rem(x + s, NX)] = ref[...]
    rows_out[...] = out_ref[...].astype(F32).reshape(64 * 16, 128)
    position = lax.broadcasted_iota(jnp.int32, (1, 256), 1).astype(F32)
    total = jnp.zeros((NX * 16, 64), F32)
    for g in range(NX):
        left = rows_in[:, :, g * 256 : (g + 1) * 256].astype(F32).reshape(NX * 16, 256)
        lens = rows_in[g, :, :128].astype(F32)[14:15, :4]
        right = []
        for h in range(2):
            cut = [
                rows_out[pl.ds((zl * 16 + core) * 16 + block * 8 + g * 2 + h, NY, stride=32), :]
                for zl in range(NZL)
                for core in range(NC)
            ]
            right.append(jnp.concatenate(cut, axis=0))
        right = jnp.concatenate(right, axis=1).astype(BF16)
        masked, start = [], jnp.zeros((1, 1), F32)
        for d in range(4):
            end = start + lens[:, d : d + 1]
            inside = (position >= start) & (position < end)
            masked.append(jnp.where(inside, left, 0.0).astype(BF16))
            start = end
        product = lax.dot_general(
            jnp.concatenate(masked, axis=0), right, (((1,), (1,)), ((), ())), preferred_element_type=F32
        )
        for d in range(4):
            one = product[d * 64 : (d + 1) * 64]
            total = total + one * one
    total = total * (1.0 / 2048.0)
    for i in range(NX):
        total_ref[i * 14 : (i + 1) * 14, :] = total[i * 16 : i * 16 + 14]


def body(acts, grads, basis_in, basis_out, doc_lengths):
    x, zh, core = lax.axis_index("x"), lax.axis_index("zh"), lax.axis_index("core")
    place = jnp.stack([x, zh, core]).astype(jnp.int32)
    tok, fin = acts.shape
    fout = grads.shape[1]
    rows = basis_in.shape[0] // NX
    tokens = NX * tok

    steps = 4
    packed, payload = pl.pallas_call(
        pack,
        out_shape=(in_hbm((CHIPS, 16, NC * (fin + fout // 2))), jax.ShapeDtypeStruct((fin + fout, tok), BF16)),
        grid=(steps,),
        in_specs=[
            SMEM,
            pl.BlockSpec((4 * rows, CHIPS * NC * fin // steps), lambda i: (0, i)),
            pl.BlockSpec((8, CHIPS * NC * fout // steps), lambda i: (0, i)),
            pl.BlockSpec((fin, tok), lambda i: (0, 0)),
            pl.BlockSpec((tok, fout), lambda i: (0, 0)),
        ],
        out_specs=(
            pl.BlockSpec((CHIPS // steps, 16, NC * (fin + fout // 2)), lambda i: (i, 0, 0)),
            pl.BlockSpec((fin + fout, tok), lambda i: (0, 0)),
        ),
        compiler_params=pltpu.CompilerParams(vmem_limit_bytes=40 << 20),
        cost_estimate=pl.CostEstimate(flops=1 << 26, bytes_accessed=5 << 20, transcendentals=0),
    )(place, from_hbm(basis_in), basis_out, acts.T, grads)
    packed = lax.all_to_all(packed, ("zl", "y"), split_axis=0, concat_axis=0, tiled=True)

    own = [payload] + [from_offset(payload, "x", NX, s) for s in range(1, NX)]
    other = [from_offset(v, "core", NC, 1) for v in own]

    parts = call(
        project,
        in_hbm((CHIPS, 16, tokens + 128)),
        [
            pltpu.VMEM((CHIPS, 16, NC * fin + fout), BF16),
            pltpu.VMEM((NC * fin, tokens), BF16),
            pltpu.VMEM((NC, fout, tokens), BF16),
            pltpu.VMEM((2 * CHIPS * 16, 128), F32),
            pltpu.VMEM((CHIPS * 16, 128), F32),
            *[pltpu.VMEM((CHIPS, 16, 256), BF16)] * NX,
            pltpu.VMEM((CHIPS, 16, 128), BF16),
            pltpu.SemaphoreType.DMA((17,)),
            pltpu.SemaphoreType.DMA((5,)),
        ],
        (place, packed, *own, *other),
        2 * 512 * 1024 * 1024,
        ANY,
    )
    parts = lax.all_to_all(parts, ("zl", "y"), split_axis=0, concat_axis=0, tiled=True)
    lens = jnp.pad(doc_lengths.astype(F32), ((0, 0), (0, 124)))
    proj_in, proj_out = call(
        add_up,
        (jax.ShapeDtypeStruct((16, tokens), BF16), in_hbm((64, 16, 128))),
        [pltpu.VMEM((16, tokens), F32), pltpu.VMEM((16, 128), F32)],
        (place, lens, in_vmem(parts)),
        32 * 16 * 1152,
    )

    proj_out = lax.all_to_all(proj_out, ("zl", "y", "core"), split_axis=0, concat_axis=0, tiled=True)
    pieces = [proj_in] + [from_offset(proj_in, "x", NX, s) for s in range(1, NX)]
    operands = (place, in_vmem(proj_out), *map(from_hbm, pieces))
    totals = [
        call(
            functools.partial(documents, which),
            jax.ShapeDtypeStruct((NX * rows, 64), F32),
            [pltpu.VMEM((NX, 16, tokens), BF16), pltpu.VMEM((64 * 16, 128), F32)],
            operands,
            2 * 4 * 256 * 256 * 64,
        )
        for which in range(NZH)
    ]
    return (totals[0] + from_offset(totals[1], "zh", NZH, 1)).T


def solution(mesh):
    fine = Mesh(mesh.devices.reshape(NX, NZH, NZL, NY, NC), ("x", "zh", "zl", "y", "core"))
    dp, mp = ("x", "zh"), ("zl", "y", "core")
    in_specs = (P(dp, mp), P(dp, mp), P(mp, None), P(mp, None), P(dp, None))
    return jax.shard_map(body, mesh=fine, in_specs=in_specs, out_specs=P(dp, mp), check_vma=False)
```

```python
import functools

import jax
import jax.numpy as jnp
from jax import lax
from jax.experimental import pallas as pl
from jax.experimental.pallas import tpu as pltpu
from jax.sharding import Mesh, PartitionSpec as P

NX, NZH, NZL, NY, NC = 4, 2, 4, 8, 2
CHIPS = NZL * NY
BF16, F32 = jnp.bfloat16, jnp.float32
SMEM = pl.BlockSpec(memory_space=pltpu.SMEM)
VMEM = pl.BlockSpec(memory_space=pltpu.VMEM)
ANY = pl.BlockSpec(memory_space=pl.ANY)


def from_offset(value, axis, size, offset):
    return lax.ppermute(value, axis, [((i + offset) % size, i) for i in range(size)])


def call(kernel, shapes, scratch, operands, flops, in_specs=None, out_spec=VMEM):
    size = sum(a.size * a.dtype.itemsize for a in operands)
    return pl.pallas_call(
        kernel,
        out_shape=shapes,
        in_specs=in_specs or [SMEM] + [VMEM] * (len(operands) - 1),
        out_specs=jax.tree.map(lambda _: out_spec, shapes),
        scratch_shapes=scratch,
        compiler_params=pltpu.CompilerParams(vmem_limit_bytes=40 << 20),
        cost_estimate=pl.CostEstimate(flops=flops, bytes_accessed=size, transcendentals=0),
    )(*operands)


def in_vmem(value):
    return pltpu.with_memory_space_constraint(value, pltpu.VMEM)


def from_hbm(value):
    return pltpu.with_memory_space_constraint(value, pltpu.HBM)


def in_hbm(shape):
    return pltpu.HBM(shape, BF16)


def pack(place, basis_ref, out_rows_ref, acts_ref, grads_ref, packed_ref, payload_ref):
    width = basis_ref.shape[1] // packed_ref.shape[0]
    fout = grads_ref.shape[1]
    for x in range(NX):

        @pl.when(place[0] == x)
        def _():
            for c in range(packed_ref.shape[0]):
                rows = basis_ref[:, c * width : (c + 1) * width].astype(F32)[x * 14 : (x + 1) * 14]
                rows = jnp.concatenate([rows, jnp.zeros((2, width), F32)], axis=0)
                packed_ref[c, :, :width] = rows.astype(BF16)

    for c in range(packed_ref.shape[0]):
        out = out_rows_ref[:, c * NC * fout : (c + 1) * NC * fout].astype(F32)
        packed_ref[c, :, width:] = jnp.concatenate([out[:, :fout], out[:, fout:]], axis=0).astype(BF16)

    @pl.when(pl.program_id(0) == 0)
    def _():
        fin = acts_ref.shape[0]
        payload_ref[:fin, :] = acts_ref[...]
        payload_ref[fin:, :] = grads_ref[...].astype(F32).T.astype(BF16)


def project(place, packed_ref, *refs):
    own, other, parts_ref = refs[:NX], refs[NX : 2 * NX], refs[2 * NX]
    acts, grads, wide, low, *outs, sems = refs[2 * NX + 1 :]
    x, core = place[0], place[2]
    fin = acts.shape[0] // NC
    fout = grads.shape[1]
    tokens, height = acts.shape[1], CHIPS * 16
    left = packed_ref[:, :, : NC * fin].reshape(height, NC * fin)
    rows_out = packed_ref[pl.ds(x * 8, 8), :, NC * fin :].astype(F32).reshape(8, NC, 8, fout)
    rows_out = [rows_out[:, c].reshape(64, fout).astype(BF16) for c in range(NC)]
    results = []
    for s in range(NX):
        cols = slice(s * 256, (s + 1) * 256)
        for pieces, which in ((own, core), (other, 1 - core)):
            acts[pl.ds(pl.multiple_of(which * fin, 16), fin), cols] = pieces[s][:fin, :]
            grads[which, :, cols] = pieces[s][fin:, :]
        part = jnp.dot(left, acts[:, cols], preferred_element_type=F32)
        out = jnp.zeros((64, 256), F32)
        for c in range(NC):
            out += jnp.dot(rows_out[c], grads[c, :, cols], preferred_element_type=F32)
        rest = out - out.astype(BF16).astype(F32)
        for h in range(2):
            block = slice(h * 128, (h + 1) * 128)
            wide[pl.ds(h * height, height), :] = part[:, block]
            for half in range(2):
                wide[pl.ds(h * height + 14 + half, CHIPS, stride=16), :] = out[half * 32 : half * 32 + 32, block]
                low[pl.ds(half * 8 + s * 2 + h, CHIPS, stride=16), :] = rest[half * 32 : half * 32 + 32, block]
            outs[s][:, :, block] = wide[h * height : (h + 1) * height].astype(BF16).reshape(CHIPS, 16, 128)
        results.append(pltpu.make_async_copy(outs[s], parts_ref.at[:, :, pl.ds(s * 256, 256)], sems.at[s]))
        results[-1].start()
    outs[NX][...] = low[...].astype(BF16).reshape(CHIPS, 16, 128)
    results.append(pltpu.make_async_copy(outs[NX], parts_ref.at[:, :, pl.ds(tokens, 128)], sems.at[NX]))
    results[-1].start()
    for result in results:
        result.wait()


def add_up(place, lens_ref, parts_ref, in_ref, out_ref, wide, narrow):
    x = place[0]
    tokens = wide.shape[1]
    total = parts_ref[0].astype(F32)
    for i in range(1, CHIPS):
        total = total + parts_ref[i].astype(F32)
    for s in range(NX):
        source = lax.rem(x + s, NX)
        wide[:, pl.ds(pl.multiple_of(source * 256, 256), 256)] = total[:, s * 256 : (s + 1) * 256]
        for half in range(2):
            for h in range(2):
                col, row = s * 2 + h, half * 8 + s * 2 + h
                value = total[14 + half : 15 + half, col * 128 : (col + 1) * 128] + total[row : row + 1, tokens:]
                narrow[pl.ds(half * 8 + source * 2 + h, 1), :] = value
    wide[14:15, :128] = lens_ref[...]
    in_ref[...] = wide[...].astype(BF16)
    rows = narrow[...]
    for half in range(NZH):
        row = rows[half * 8 : half * 8 + 8].astype(BF16)
        out_ref[half * 64 : (half + 1) * 64] = jnp.broadcast_to(row[None], (64, 8, 128))


def documents(place, out_ref, *refs):
    pieces, (total_ref, rows_in, rows_out, sems) = refs[:NX], refs[NX:]
    x, zh = place[0], place[1]
    copies = []
    for s in range(NX):
        for half in range(NZH):
            there = rows_in.at[lax.rem(x + s, NX), lax.rem(half + zh, NZH)]
            copies.append(pltpu.make_async_copy(pieces[s].at[half], there, sems.at[s * NZH + half]))
            copies[-1].start()
    rows_out[...] = out_ref[...].astype(F32).reshape(128 * 8, 128)
    position = lax.broadcasted_iota(jnp.int32, (1, 256), 1).astype(F32)
    for copy in copies:
        copy.wait()
    total = jnp.zeros((NX * 16, 64), F32)
    for half in range(NZH):
        for g in range(NX):
            left = rows_in[:, half, :, g * 256 : (g + 1) * 256].astype(F32).reshape(NX * 16, 256)
            lens = rows_in[g, half, :, :128].astype(F32)[14:15, :4]
            right = []
            for h in range(2):
                cut = [
                    rows_out[pl.ds((half * 64 + zl * 16 + core) * 8 + g * 2 + h, NY, stride=16), :]
                    for zl in range(NZL)
                    for core in range(NC)
                ]
                right.append(jnp.concatenate(cut, axis=0))
            right = jnp.concatenate(right, axis=1).astype(BF16)
            masked, start = [], jnp.zeros((1, 1), F32)
            for d in range(4):
                end = start + lens[:, d : d + 1]
                inside = (position >= start) & (position < end)
                masked.append(jnp.where(inside, left, 0.0).astype(BF16))
                start = end
            product = lax.dot_general(
                jnp.concatenate(masked, axis=0), right, (((1,), (1,)), ((), ())), preferred_element_type=F32
            )
            for d in range(4):
                one = product[d * 64 : (d + 1) * 64]
                total = total + one * one
    total = total * (1.0 / 2048.0)
    for i in range(NX):
        total_ref[i * 14 : (i + 1) * 14, :] = total[i * 16 : i * 16 + 14]


def body(acts, grads, basis_in, basis_out, doc_lengths):
    x, zh, core = lax.axis_index("x"), lax.axis_index("zh"), lax.axis_index("core")
    place = jnp.stack([x, zh, core]).astype(jnp.int32)
    tok, fin = acts.shape
    fout = grads.shape[1]
    rows = basis_in.shape[0] // NX
    tokens = NX * tok

    steps = 4
    packed, payload = pl.pallas_call(
        pack,
        out_shape=(in_hbm((CHIPS, 16, NC * (fin + fout // 2))), jax.ShapeDtypeStruct((fin + fout, tok), BF16)),
        grid=(steps,),
        in_specs=[
            SMEM,
            pl.BlockSpec((4 * rows, CHIPS * NC * fin // steps), lambda i: (0, i)),
            pl.BlockSpec((8, CHIPS * NC * fout // steps), lambda i: (0, i)),
            pl.BlockSpec((fin, tok), lambda i: (0, 0)),
            pl.BlockSpec((tok, fout), lambda i: (0, 0)),
        ],
        out_specs=(
            pl.BlockSpec((CHIPS // steps, 16, NC * (fin + fout // 2)), lambda i: (i, 0, 0)),
            pl.BlockSpec((fin + fout, tok), lambda i: (0, 0)),
        ),
        compiler_params=pltpu.CompilerParams(vmem_limit_bytes=40 << 20),
        cost_estimate=pl.CostEstimate(flops=1 << 26, bytes_accessed=5 << 20, transcendentals=0),
    )(place, *map(from_hbm, (basis_in, basis_out, acts.T, grads)))
    packed = lax.all_to_all(packed, ("zl", "y"), split_axis=0, concat_axis=0, tiled=True)

    own = [payload] + [from_offset(payload, "x", NX, s) for s in range(1, NX)]
    other = [from_offset(v, "core", NC, 1) for v in own]

    parts = call(
        project,
        in_hbm((CHIPS, 16, tokens + 128)),
        [
            pltpu.VMEM((NC * fin, tokens), BF16),
            pltpu.VMEM((NC, fout, tokens), BF16),
            pltpu.VMEM((2 * CHIPS * 16, 128), F32),
            pltpu.VMEM((CHIPS * 16, 128), F32),
            *[pltpu.VMEM((CHIPS, 16, 256), BF16)] * NX,
            pltpu.VMEM((CHIPS, 16, 128), BF16),
            pltpu.SemaphoreType.DMA((5,)),
        ],
        (place, *map(in_vmem, (packed, *own, *other))),
        2 * 512 * 1024 * 1024,
        out_spec=ANY,
    )
    parts = lax.all_to_all(parts, ("zl", "y"), split_axis=0, concat_axis=0, tiled=True)
    lens = jnp.pad(doc_lengths.astype(F32), ((0, 0), (0, 124)))
    proj_in, proj_out = call(
        add_up,
        (jax.ShapeDtypeStruct((16, tokens), BF16), in_hbm((128, 8, 128))),
        [pltpu.VMEM((16, tokens), F32), pltpu.VMEM((16, 128), F32)],
        (place, lens, in_vmem(parts)),
        32 * 16 * 1152,
    )

    pair = jnp.stack([proj_in, from_offset(proj_in, "zh", NZH, 1)])
    proj_out = lax.all_to_all(proj_out, ("zh", "zl", "y", "core"), split_axis=0, concat_axis=0, tiled=True)
    pieces = [pair] + [from_offset(pair, "x", NX, s) for s in range(1, NX)]
    total = call(
        documents,
        jax.ShapeDtypeStruct((NX * rows, 64), F32),
        [
            pltpu.VMEM((NX, NZH, 16, tokens), BF16),
            pltpu.VMEM((128 * 8, 128), F32),
            pltpu.SemaphoreType.DMA((NX * NZH,)),
        ],
        (place, in_vmem(proj_out), *pieces),
        2 * 8 * 256 * 256 * 64,
        in_specs=[SMEM, VMEM] + [ANY] * NX,
    )
    return total.T


def solution(mesh):
    fine = Mesh(mesh.devices.reshape(NX, NZH, NZL, NY, NC), ("x", "zh", "zl", "y", "core"))
    dp, mp = ("x", "zh"), ("zl", "y", "core")
    in_specs = (P(dp, mp), P(dp, mp), P(mp, None), P(mp, None), P(dp, None))
    return jax.shard_map(body, mesh=fine, in_specs=in_specs, out_specs=P(dp, mp), check_vma=False)
```

```python
import functools

import jax
import jax.numpy as jnp
from jax import lax
from jax.experimental import pallas as pl
from jax.experimental.pallas import tpu as pltpu
from jax.sharding import Mesh, PartitionSpec as P

NX, NZH, NZL, NY, NC = 4, 2, 4, 8, 2
CHIPS = NZL * NY
PARTS = 8
BF16, F32 = jnp.bfloat16, jnp.float32
SMEM = pl.BlockSpec(memory_space=pltpu.SMEM)
VMEM = pl.BlockSpec(memory_space=pltpu.VMEM)
ANY = pl.BlockSpec(memory_space=pl.ANY)


def from_offset(value, axis, size, offset):
    return lax.ppermute(value, axis, [((i + offset) % size, i) for i in range(size)])


def call(kernel, shapes, scratch, operands, flops, in_specs=None, out_spec=VMEM):
    size = sum(a.size * a.dtype.itemsize for a in operands)
    return pl.pallas_call(
        kernel,
        out_shape=shapes,
        in_specs=in_specs or [SMEM] + [VMEM] * (len(operands) - 1),
        out_specs=jax.tree.map(lambda _: out_spec, shapes),
        scratch_shapes=scratch,
        compiler_params=pltpu.CompilerParams(vmem_limit_bytes=40 << 20),
        cost_estimate=pl.CostEstimate(flops=flops, bytes_accessed=size, transcendentals=0),
    )(*operands)


def in_vmem(value):
    return pltpu.with_memory_space_constraint(value, pltpu.VMEM)


def from_hbm(value):
    return pltpu.with_memory_space_constraint(value, pltpu.HBM)


def in_hbm(shape):
    return pltpu.HBM(shape, BF16)


def pack(place, basis_ref, out_rows_ref, acts_ref, grads_ref, packed_ref, payload_ref, *scratch):
    basis, out_rows, grads, turned, packed, sems = scratch
    fin, fout = acts_ref.shape[0], grads_ref.shape[1]
    width, chips = NC * fin, CHIPS // PARTS
    loads = [
        pltpu.make_async_copy(out_rows_ref, out_rows, sems.at[0]),
        pltpu.make_async_copy(grads_ref, grads, sems.at[1]),
    ]
    for i in range(PARTS):
        cols = pl.ds(i * chips * width, chips * width)
        loads.append(pltpu.make_async_copy(basis_ref.at[:, cols], basis.at[i], sems.at[2 + i]))
    stores = [pltpu.make_async_copy(acts_ref, payload_ref.at[pl.ds(0, fin)], sems.at[2 + PARTS])]
    for copy in loads + stores:
        copy.start()
    loads[0].wait()
    for c in range(CHIPS):
        out = out_rows[:, c * NC * fout : (c + 1) * NC * fout].astype(F32)
        out = jnp.concatenate([out[:, :fout], out[:, fout:]], axis=0).astype(BF16)
        packed[c // chips, c % chips, :, width:] = out
    loads[1].wait()
    turned[...] = grads[...].astype(F32).T.astype(BF16)
    stores.append(pltpu.make_async_copy(turned, payload_ref.at[pl.ds(fin, fout)], sems.at[3 + PARTS]))
    stores[-1].start()
    for i in range(PARTS):
        loads[2 + i].wait()
        for x in range(NX):

            @pl.when(place[0] == x)
            def _():
                for c in range(chips):
                    rows = basis[i, :, c * width : (c + 1) * width].astype(F32)[x * 14 : (x + 1) * 14]
                    rows = jnp.concatenate([rows, jnp.zeros((2, width), F32)], axis=0)
                    packed[i, c, :, :width] = rows.astype(BF16)

        there = packed_ref.at[pl.ds(i * chips, chips)]
        stores.append(pltpu.make_async_copy(packed.at[i], there, sems.at[4 + PARTS + i]))
        stores[-1].start()
    for store in stores:
        store.wait()


def project(place, packed_ref, *refs):
    own, other, parts_ref = refs[:NX], refs[NX : 2 * NX], refs[2 * NX]
    acts, grads, wide, low, *outs, sems = refs[2 * NX + 1 :]
    x, core = place[0], place[2]
    fin = acts.shape[0] // NC
    fout = grads.shape[1]
    tokens, height = acts.shape[1], CHIPS * 16
    left = packed_ref[:, :, : NC * fin].reshape(height, NC * fin)
    rows_out = packed_ref[pl.ds(x * 8, 8), :, NC * fin :].astype(F32).reshape(8, NC, 8, fout)
    rows_out = [rows_out[:, c].reshape(64, fout).astype(BF16) for c in range(NC)]
    results = []
    for s in range(NX):
        cols = slice(s * 256, (s + 1) * 256)
        for pieces, which in ((own, core), (other, 1 - core)):
            acts[pl.ds(pl.multiple_of(which * fin, 16), fin), cols] = pieces[s][:fin, :]
            grads[which, :, cols] = pieces[s][fin:, :]
        part = jnp.dot(left, acts[:, cols], preferred_element_type=F32)
        out = jnp.zeros((64, 256), F32)
        for c in range(NC):
            out += jnp.dot(rows_out[c], grads[c, :, cols], preferred_element_type=F32)
        rest = out - out.astype(BF16).astype(F32)
        for h in range(2):
            block = slice(h * 128, (h + 1) * 128)
            wide[pl.ds(h * height, height), :] = part[:, block]
            for half in range(2):
                wide[pl.ds(h * height + 14 + half, CHIPS, stride=16), :] = out[half * 32 : half * 32 + 32, block]
                low[pl.ds(half * 8 + s * 2 + h, CHIPS, stride=16), :] = rest[half * 32 : half * 32 + 32, block]
            outs[s][:, :, block] = wide[h * height : (h + 1) * height].astype(BF16).reshape(CHIPS, 16, 128)
        results.append(pltpu.make_async_copy(outs[s], parts_ref.at[:, :, pl.ds(s * 256, 256)], sems.at[s]))
        results[-1].start()
    outs[NX][...] = low[...].astype(BF16).reshape(CHIPS, 16, 128)
    results.append(pltpu.make_async_copy(outs[NX], parts_ref.at[:, :, pl.ds(tokens, 128)], sems.at[NX]))
    results[-1].start()
    for result in results:
        result.wait()


def add_up(place, lens_ref, parts_ref, in_ref, out_ref, wide, narrow):
    x = place[0]
    tokens = wide.shape[1]
    total = parts_ref[0].astype(F32)
    for i in range(1, CHIPS):
        total = total + parts_ref[i].astype(F32)
    for s in range(NX):
        source = lax.rem(x + s, NX)
        wide[:, pl.ds(pl.multiple_of(source * 256, 256), 256)] = total[:, s * 256 : (s + 1) * 256]
        for half in range(2):
            for h in range(2):
                col, row = s * 2 + h, half * 8 + s * 2 + h
                value = total[14 + half : 15 + half, col * 128 : (col + 1) * 128] + total[row : row + 1, tokens:]
                narrow[pl.ds(half * 8 + source * 2 + h, 1), :] = value
    wide[14:15, :128] = lens_ref[...]
    in_ref[...] = wide[...].astype(BF16)
    out_ref[...] = jnp.broadcast_to(narrow[...].astype(BF16)[None], out_ref.shape)


def documents(which, place, out_ref, *refs):
    pieces, (total_ref, rows_in, rows_out, sems) = refs[:NX], refs[NX:]
    x, zh = place[0], place[1]
    block = lax.rem(zh + which, NZH)
    copies = []
    for s in range(NX):
        copies.append(pltpu.make_async_copy(pieces[s], rows_in.at[lax.rem(x + s, NX)], sems.at[s]))
        copies[-1].start()
    rows_out[...] = out_ref[...].astype(F32).reshape(64 * 16, 128)
    position = lax.broadcasted_iota(jnp.int32, (1, 256), 1).astype(F32)
    for copy in copies:
        copy.wait()
    total = jnp.zeros((NX * 16, 64), F32)
    for g in range(NX):
        left = rows_in[:, :, g * 256 : (g + 1) * 256].astype(F32).reshape(NX * 16, 256)
        lens = rows_in[g, :, :128].astype(F32)[14:15, :4]
        right = []
        for h in range(2):
            cut = [
                rows_out[pl.ds((zl * 16 + core) * 16 + block * 8 + g * 2 + h, NY, stride=32), :]
                for zl in range(NZL)
                for core in range(NC)
            ]
            right.append(jnp.concatenate(cut, axis=0))
        right = jnp.concatenate(right, axis=1).astype(BF16)
        masked, start = [], jnp.zeros((1, 1), F32)
        for d in range(4):
            end = start + lens[:, d : d + 1]
            inside = (position >= start) & (position < end)
            masked.append(jnp.where(inside, left, 0.0).astype(BF16))
            start = end
        product = lax.dot_general(
            jnp.concatenate(masked, axis=0), right, (((1,), (1,)), ((), ())), preferred_element_type=F32
        )
        for d in range(4):
            one = product[d * 64 : (d + 1) * 64]
            total = total + one * one
    total = total * (1.0 / 2048.0)
    for i in range(NX):
        total_ref[i * 14 : (i + 1) * 14, :] = total[i * 16 : i * 16 + 14]


def body(acts, grads, basis_in, basis_out, doc_lengths):
    x, zh, core = lax.axis_index("x"), lax.axis_index("zh"), lax.axis_index("core")
    place = jnp.stack([x, zh, core]).astype(jnp.int32)
    tok, fin = acts.shape
    fout = grads.shape[1]
    rows = basis_in.shape[0] // NX
    tokens = NX * tok

    packed, payload = call(
        pack,
        (in_hbm((CHIPS, 16, NC * fin + fout)), jax.ShapeDtypeStruct((fin + fout, tok), BF16)),
        [
            pltpu.VMEM((PARTS, 4 * rows, CHIPS // PARTS * NC * fin), BF16),
            pltpu.VMEM((8, CHIPS * NC * fout), BF16),
            pltpu.VMEM((tok, fout), BF16),
            pltpu.VMEM((fout, tok), BF16),
            pltpu.VMEM((PARTS, CHIPS // PARTS, 16, NC * fin + fout), BF16),
            pltpu.SemaphoreType.DMA((2 * PARTS + 4,)),
        ],
        (place, *map(from_hbm, (basis_in, basis_out, acts.T, grads))),
        1 << 20,
        in_specs=[SMEM] + [ANY] * 4,
        out_spec=ANY,
    )
    packed = lax.all_to_all(packed, ("zl", "y"), split_axis=0, concat_axis=0, tiled=True)

    own = [payload] + [from_offset(payload, "x", NX, s) for s in range(1, NX)]
    other = [from_offset(v, "core", NC, 1) for v in own]

    parts = call(
        project,
        in_hbm((CHIPS, 16, tokens + 128)),
        [
            pltpu.VMEM((NC * fin, tokens), BF16),
            pltpu.VMEM((NC, fout, tokens), BF16),
            pltpu.VMEM((2 * CHIPS * 16, 128), F32),
            pltpu.VMEM((CHIPS * 16, 128), F32),
            *[pltpu.VMEM((CHIPS, 16, 256), BF16)] * NX,
            pltpu.VMEM((CHIPS, 16, 128), BF16),
            pltpu.SemaphoreType.DMA((5,)),
        ],
        (place, *map(in_vmem, (packed, *own, *other))),
        2 * 512 * 1024 * 1024,
        out_spec=ANY,
    )
    parts = lax.all_to_all(parts, ("zl", "y"), split_axis=0, concat_axis=0, tiled=True)
    lens = jnp.pad(doc_lengths.astype(F32), ((0, 0), (0, 124)))
    proj_in, proj_out = call(
        add_up,
        (jax.ShapeDtypeStruct((16, tokens), BF16), in_hbm((64, 16, 128))),
        [pltpu.VMEM((16, tokens), F32), pltpu.VMEM((16, 128), F32)],
        (place, lens, in_vmem(parts)),
        32 * 16 * 1152,
    )

    proj_out = lax.all_to_all(proj_out, ("zl", "y", "core"), split_axis=0, concat_axis=0, tiled=True)
    pieces = [proj_in] + [from_offset(proj_in, "x", NX, s) for s in range(1, NX)]
    operands = (place, in_vmem(proj_out), *pieces)
    totals = [
        call(
            functools.partial(documents, which),
            jax.ShapeDtypeStruct((NX * rows, 64), F32),
            [
                pltpu.VMEM((NX, 16, tokens), BF16),
                pltpu.VMEM((64 * 16, 128), F32),
                pltpu.SemaphoreType.DMA((NX,)),
            ],
            operands,
            2 * 4 * 256 * 256 * 64,
            in_specs=[SMEM, VMEM] + [ANY] * NX,
        )
        for which in range(NZH)
    ]
    return (totals[0] + from_offset(totals[1], "zh", NZH, 1)).T


def solution(mesh):
    fine = Mesh(mesh.devices.reshape(NX, NZH, NZL, NY, NC), ("x", "zh", "zl", "y", "core"))
    dp, mp = ("x", "zh"), ("zl", "y", "core")
    in_specs = (P(dp, mp), P(dp, mp), P(mp, None), P(mp, None), P(dp, None))
    return jax.shard_map(body, mesh=fine, in_specs=in_specs, out_specs=P(dp, mp), check_vma=False)
```

```python
import functools

import jax
import jax.numpy as jnp
from jax import lax
from jax.experimental import pallas as pl
from jax.experimental.pallas import tpu as pltpu
from jax.sharding import Mesh, PartitionSpec as P

NX, NZH, NZL, NY, NC = 4, 2, 4, 8, 2
CHIPS = NZL * NY
PARTS = 8
BF16, F32 = jnp.bfloat16, jnp.float32
SMEM = pl.BlockSpec(memory_space=pltpu.SMEM)
VMEM = pl.BlockSpec(memory_space=pltpu.VMEM)
ANY = pl.BlockSpec(memory_space=pl.ANY)


def from_offset(value, axis, size, offset):
    return lax.ppermute(value, axis, [((i + offset) % size, i) for i in range(size)])


def call(kernel, shapes, scratch, operands, flops, in_specs=None, out_spec=VMEM):
    size = sum(a.size * a.dtype.itemsize for a in operands)
    return pl.pallas_call(
        kernel,
        out_shape=shapes,
        in_specs=in_specs or [SMEM] + [VMEM] * (len(operands) - 1),
        out_specs=jax.tree.map(lambda _: out_spec, shapes),
        scratch_shapes=scratch,
        compiler_params=pltpu.CompilerParams(vmem_limit_bytes=40 << 20),
        cost_estimate=pl.CostEstimate(flops=flops, bytes_accessed=size, transcendentals=0),
    )(*operands)


def in_vmem(value):
    return pltpu.with_memory_space_constraint(value, pltpu.VMEM)


def from_hbm(value):
    return pltpu.with_memory_space_constraint(value, pltpu.HBM)


def in_hbm(shape):
    return pltpu.HBM(shape, BF16)


def pack(place, basis_ref, out_rows_ref, acts_ref, grads_ref, packed_ref, payload_ref, *scratch):
    basis, out_rows, grads, turned, packed, sems = scratch
    fin, fout = acts_ref.shape[0], grads_ref.shape[1]
    width, chips = NC * fin, CHIPS // PARTS
    loads = [
        pltpu.make_async_copy(out_rows_ref, out_rows, sems.at[0]),
        pltpu.make_async_copy(grads_ref, grads, sems.at[1]),
    ]
    for i in range(PARTS):
        cols = pl.ds(i * chips * width, chips * width)
        loads.append(pltpu.make_async_copy(basis_ref.at[:, cols], basis.at[i], sems.at[2 + i]))
    stores = [pltpu.make_async_copy(acts_ref, payload_ref.at[pl.ds(0, fin)], sems.at[2 + PARTS])]
    for copy in loads + stores:
        copy.start()
    loads[0].wait()
    for c in range(CHIPS):
        out = out_rows[:, c * NC * fout : (c + 1) * NC * fout].astype(F32)
        out = jnp.concatenate([out[:, :fout], out[:, fout:]], axis=0).astype(BF16)
        packed[c // chips, c % chips, :, width:] = out
    loads[1].wait()
    turned[...] = grads[...].astype(F32).T.astype(BF16)
    stores.append(pltpu.make_async_copy(turned, payload_ref.at[pl.ds(fin, fout)], sems.at[3 + PARTS]))
    stores[-1].start()
    for i in range(PARTS):
        loads[2 + i].wait()
        for x in range(NX):

            @pl.when(place[0] == x)
            def _():
                for c in range(chips):
                    rows = basis[i, :, c * width : (c + 1) * width].astype(F32)[x * 14 : (x + 1) * 14]
                    rows = jnp.concatenate([rows, jnp.zeros((2, width), F32)], axis=0)
                    packed[i, c, :, :width] = rows.astype(BF16)

        there = packed_ref.at[pl.ds(i * chips, chips)]
        stores.append(pltpu.make_async_copy(packed.at[i], there, sems.at[4 + PARTS + i]))
        stores[-1].start()
    for store in stores:
        store.wait()


def project(place, packed_ref, *refs):
    own, other, parts_ref = refs[:NX], refs[NX : 2 * NX], refs[2 * NX]
    acts, grads, wide, low, *outs, sems = refs[2 * NX + 1 :]
    x, core = place[0], place[2]
    fin = acts.shape[0] // NC
    fout = grads.shape[1]
    tokens, height = acts.shape[1], CHIPS * 16
    left = packed_ref[:, :, : NC * fin].reshape(height, NC * fin)
    rows_out = packed_ref[pl.ds(x * 8, 8), :, NC * fin :].astype(F32).reshape(8, NC, 8, fout)
    rows_out = [rows_out[:, c].reshape(64, fout).astype(BF16) for c in range(NC)]
    results = []
    for s in range(NX):
        cols = slice(s * 256, (s + 1) * 256)
        for pieces, which in ((own, core), (other, 1 - core)):
            acts[pl.ds(pl.multiple_of(which * fin, 16), fin), cols] = pieces[s][:fin, :]
            grads[which, :, cols] = pieces[s][fin:, :]
        part = jnp.dot(left, acts[:, cols], preferred_element_type=F32)
        out = jnp.zeros((64, 256), F32)
        for c in range(NC):
            out += jnp.dot(rows_out[c], grads[c, :, cols], preferred_element_type=F32)
        rest = out - out.astype(BF16).astype(F32)
        for h in range(2):
            block = slice(h * 128, (h + 1) * 128)
            wide[pl.ds(h * height, height), :] = part[:, block]
            for half in range(2):
                wide[pl.ds(h * height + 14 + half, CHIPS, stride=16), :] = out[half * 32 : half * 32 + 32, block]
                low[pl.ds(half * 8 + s * 2 + h, CHIPS, stride=16), :] = rest[half * 32 : half * 32 + 32, block]
            outs[s][:, :, block] = wide[h * height : (h + 1) * height].astype(BF16).reshape(CHIPS, 16, 128)
        results.append(pltpu.make_async_copy(outs[s], parts_ref.at[:, :, pl.ds(s * 256, 256)], sems.at[s]))
        results[-1].start()
    outs[NX][...] = low[...].astype(BF16).reshape(CHIPS, 16, 128)
    results.append(pltpu.make_async_copy(outs[NX], parts_ref.at[:, :, pl.ds(tokens, 128)], sems.at[NX]))
    results[-1].start()
    for result in results:
        result.wait()


def add_up(place, lens_ref, parts_ref, in_ref, out_ref, wide, narrow):
    x = place[0]
    tokens = wide.shape[1]
    total = parts_ref[0].astype(F32)
    for i in range(1, CHIPS):
        total = total + parts_ref[i].astype(F32)
    for s in range(NX):
        source = lax.rem(x + s, NX)
        wide[:, pl.ds(pl.multiple_of(source * 256, 256), 256)] = total[:, s * 256 : (s + 1) * 256]
        for half in range(2):
            for h in range(2):
                col, row = s * 2 + h, half * 8 + s * 2 + h
                value = total[14 + half : 15 + half, col * 128 : (col + 1) * 128] + total[row : row + 1, tokens:]
                narrow[pl.ds(half * 8 + source * 2 + h, 1), :] = value
    wide[14:15, :128] = lens_ref[...]
    in_ref[...] = wide[...].astype(BF16)
    out_ref[...] = jnp.broadcast_to(narrow[...].astype(BF16)[None], out_ref.shape)


def documents(which, place, out_ref, *refs):
    pairs, (total_ref, rows_in, rows_out, sems) = refs[:2], refs[2:]
    x, zh = place[0], place[1]
    block = lax.rem(zh + which, NZH)
    near = x + 1 - 2 * lax.rem(x, 2)
    copies = []
    for s, source in enumerate((x, near, NX - 1 - x, NX - 1 - near)):
        copies.append(pltpu.make_async_copy(pairs[s // 2].at[s % 2], rows_in.at[source], sems.at[s]))
        copies[-1].start()
    rows_out[...] = out_ref[...].astype(F32).reshape(64 * 16, 128)
    position = lax.broadcasted_iota(jnp.int32, (1, 256), 1).astype(F32)
    for copy in copies:
        copy.wait()
    total = jnp.zeros((NX * 16, 64), F32)
    for g in range(NX):
        left = rows_in[:, :, g * 256 : (g + 1) * 256].astype(F32).reshape(NX * 16, 256)
        lens = rows_in[g, :, :128].astype(F32)[14:15, :4]
        right = []
        for h in range(2):
            cut = [
                rows_out[pl.ds(i * NY * 16 + block * 8 + g * 2 + h, NY, stride=16), :]
                for i in range(NZL * NC)
            ]
            right.append(jnp.concatenate(cut, axis=0))
        right = jnp.concatenate(right, axis=1).astype(BF16)
        masked, start = [], jnp.zeros((1, 1), F32)
        for d in range(4):
            end = start + lens[:, d : d + 1]
            inside = (position >= start) & (position < end)
            masked.append(jnp.where(inside, left, 0.0).astype(BF16))
            start = end
        product = lax.dot_general(
            jnp.concatenate(masked, axis=0), right, (((1,), (1,)), ((), ())), preferred_element_type=F32
        )
        for d in range(4):
            one = product[d * 64 : (d + 1) * 64]
            total = total + one * one
    total = total * (1.0 / 2048.0)
    for i in range(NX):
        total_ref[i * 14 : (i + 1) * 14, :] = total[i * 16 : i * 16 + 14]


def body(acts, grads, basis_in, basis_out, doc_lengths):
    x, zh, core = lax.axis_index("x"), lax.axis_index("zh"), lax.axis_index("core")
    place = jnp.stack([x, zh, core]).astype(jnp.int32)
    tok, fin = acts.shape
    fout = grads.shape[1]
    rows = basis_in.shape[0] // NX
    tokens = NX * tok

    packed, payload = call(
        pack,
        (in_hbm((CHIPS, 16, NC * fin + fout)), jax.ShapeDtypeStruct((fin + fout, tok), BF16)),
        [
            pltpu.VMEM((PARTS, 4 * rows, CHIPS // PARTS * NC * fin), BF16),
            pltpu.VMEM((8, CHIPS * NC * fout), BF16),
            pltpu.VMEM((tok, fout), BF16),
            pltpu.VMEM((fout, tok), BF16),
            pltpu.VMEM((PARTS, CHIPS // PARTS, 16, NC * fin + fout), BF16),
            pltpu.SemaphoreType.DMA((2 * PARTS + 4,)),
        ],
        (place, *map(from_hbm, (basis_in, basis_out, acts.T, grads))),
        1 << 20,
        in_specs=[SMEM] + [ANY] * 4,
        out_spec=ANY,
    )
    packed = lax.all_to_all(packed, ("zl", "y"), split_axis=0, concat_axis=0, tiled=True)

    own = [payload] + [from_offset(payload, "x", NX, s) for s in range(1, NX)]
    other = [from_offset(v, "core", NC, 1) for v in own]

    parts = call(
        project,
        in_hbm((CHIPS, 16, tokens + 128)),
        [
            pltpu.VMEM((NC * fin, tokens), BF16),
            pltpu.VMEM((NC, fout, tokens), BF16),
            pltpu.VMEM((2 * CHIPS * 16, 128), F32),
            pltpu.VMEM((CHIPS * 16, 128), F32),
            *[pltpu.VMEM((CHIPS, 16, 256), BF16)] * NX,
            pltpu.VMEM((CHIPS, 16, 128), BF16),
            pltpu.SemaphoreType.DMA((5,)),
        ],
        (place, *map(in_vmem, (packed, *own, *other))),
        2 * 512 * 1024 * 1024,
        out_spec=ANY,
    )
    parts = lax.all_to_all(parts, ("zl", "y"), split_axis=0, concat_axis=0, tiled=True)
    lens = jnp.pad(doc_lengths.astype(F32), ((0, 0), (0, 124)))
    proj_in, proj_out = call(
        add_up,
        (jax.ShapeDtypeStruct((16, tokens), BF16), in_hbm((NY, 16, 128))),
        [pltpu.VMEM((16, tokens), F32), pltpu.VMEM((16, 128), F32)],
        (place, lens, in_vmem(parts)),
        32 * 16 * 1152,
    )

    proj_out = lax.all_to_all(proj_out, "y", split_axis=0, concat_axis=0, tiled=True)
    proj_out = jnp.broadcast_to(proj_out[None], (NZL * NC, NY, 16, 128)).reshape(64, 16, 128)
    proj_out = lax.all_to_all(proj_out, ("zl", "core"), split_axis=0, concat_axis=0, tiled=True)
    pair = jnp.stack([proj_in, lax.ppermute(proj_in, "x", [(0, 1), (1, 0), (2, 3), (3, 2)])])
    far = lax.ppermute(pair, "x", [(0, 3), (3, 0), (1, 2), (2, 1)])
    operands = (place, in_vmem(proj_out), pair, far)
    totals = [
        call(
            functools.partial(documents, which),
            jax.ShapeDtypeStruct((NX * rows, 64), F32),
            [
                pltpu.VMEM((NX, 16, tokens), BF16),
                pltpu.VMEM((64 * 16, 128), F32),
                pltpu.SemaphoreType.DMA((NX,)),
            ],
            operands,
            2 * 4 * 256 * 256 * 64,
            in_specs=[SMEM, VMEM, ANY, ANY],
        )
        for which in range(NZH)
    ]
    return (totals[0] + from_offset(totals[1], "zh", NZH, 1)).T


def solution(mesh):
    fine = Mesh(mesh.devices.reshape(NX, NZH, NZL, NY, NC), ("x", "zh", "zl", "y", "core"))
    dp, mp = ("x", "zh"), ("zl", "y", "core")
    in_specs = (P(dp, mp), P(dp, mp), P(mp, None), P(mp, None), P(dp, None))
    return jax.shard_map(body, mesh=fine, in_specs=in_specs, out_specs=P(dp, mp), check_vma=False)
```

```python
import functools

import jax
import jax.numpy as jnp
from jax import lax
from jax.experimental import pallas as pl
from jax.experimental.pallas import tpu as pltpu
from jax.sharding import Mesh, PartitionSpec as P

NX, NZH, NZL, NY, NC = 4, 2, 4, 8, 2
CHIPS = NZL * NY
PARTS = 8
BF16, F32 = jnp.bfloat16, jnp.float32
SMEM = pl.BlockSpec(memory_space=pltpu.SMEM)
VMEM = pl.BlockSpec(memory_space=pltpu.VMEM)
ANY = pl.BlockSpec(memory_space=pl.ANY)


def from_offset(value, axis, size, offset):
    return lax.ppermute(value, axis, [((i + offset) % size, i) for i in range(size)])


def call(kernel, shapes, scratch, operands, flops, in_specs=None, out_spec=VMEM):
    size = sum(a.size * a.dtype.itemsize for a in operands)
    return pl.pallas_call(
        kernel,
        out_shape=shapes,
        in_specs=in_specs or [SMEM] + [VMEM] * (len(operands) - 1),
        out_specs=jax.tree.map(lambda _: out_spec, shapes),
        scratch_shapes=scratch,
        compiler_params=pltpu.CompilerParams(vmem_limit_bytes=40 << 20),
        cost_estimate=pl.CostEstimate(flops=flops, bytes_accessed=size, transcendentals=0),
    )(*operands)


def in_vmem(value):
    return pltpu.with_memory_space_constraint(value, pltpu.VMEM)


def from_hbm(value):
    return pltpu.with_memory_space_constraint(value, pltpu.HBM)


def in_hbm(shape):
    return pltpu.HBM(shape, BF16)


def pack(place, basis_ref, out_rows_ref, grads_ref, packed_ref, turned_ref, *scratch):
    basis, out_rows, grads, turned, packed, sems = scratch
    fout = grads_ref.shape[1]
    fin = basis_ref.shape[1] // (CHIPS * NC)
    width, chips = NC * fin, CHIPS // PARTS
    loads = [
        pltpu.make_async_copy(out_rows_ref, out_rows, sems.at[0]),
        pltpu.make_async_copy(grads_ref, grads, sems.at[1]),
    ]
    for i in range(PARTS):
        cols = pl.ds(i * chips * width, chips * width)
        loads.append(pltpu.make_async_copy(basis_ref.at[:, cols], basis.at[i], sems.at[2 + i]))
    for load in loads:
        load.start()
    loads[0].wait()
    for c in range(CHIPS):
        half = c // NY % 2
        rows = out_rows[:, (c - half * NY) * NC * fout : (c - half * NY + 1) * NC * fout].astype(F32)
        more = out_rows[:, (c - half * NY + NY) * NC * fout : (c - half * NY + NY + 1) * NC * fout].astype(F32)
        blocks = [v[half * 4 : half * 4 + 4, k * fout : (k + 1) * fout] for v in (rows, more) for k in range(NC)]
        packed[c // chips, c % chips, :, width:] = jnp.concatenate(blocks, axis=0).astype(BF16)
    loads[1].wait()
    turned[...] = grads[...].astype(F32).T.astype(BF16)
    stores = [pltpu.make_async_copy(turned, turned_ref, sems.at[3 + PARTS])]
    stores[0].start()
    for i in range(PARTS):
        loads[2 + i].wait()
        for x in range(NX):

            @pl.when(place[0] == x)
            def _():
                for c in range(chips):
                    rows = basis[i, :, c * width : (c + 1) * width].astype(F32)[x * 14 : (x + 1) * 14]
                    rows = jnp.concatenate([rows, jnp.zeros((2, width), F32)], axis=0)
                    packed[i, c, :, :width] = rows.astype(BF16)

        there = packed_ref.at[pl.ds(i * chips, chips)]
        stores.append(pltpu.make_async_copy(packed.at[i], there, sems.at[4 + PARTS + i]))
        stores[-1].start()
    for store in stores:
        store.wait()


def project(place, packed_ref, *refs):
    own, other, parts_ref = refs[:NX], refs[NX : 2 * NX], refs[2 * NX]
    acts, grads, thin, wide, *outs, sems = refs[2 * NX + 1 :]
    x, core, odd = place[0], place[2], place[3]
    fin = acts.shape[0] // NC
    fout = grads.shape[1]
    height = CHIPS * 16
    left = packed_ref[:, :, : NC * fin].reshape(height, NC * fin)
    thin[...] = packed_ref[pl.ds(x * NY, NY), :, NC * fin :].astype(F32).reshape(NY * 16, fout)
    rows_out = []
    for k in range(2 * NC):
        cut = [thin[pl.ds(k * 4 + i, NY, stride=16), :] for i in range(4)]
        rows_out.append(jnp.concatenate(cut, axis=0).astype(BF16))
    results = []
    for s in range(NX):
        cols = slice(s * 256, (s + 1) * 256)
        for pieces, which in ((own, core), (other, 1 - core)):
            acts[pl.ds(pl.multiple_of(which * fin, 16), fin), cols] = pieces[s][:fin, :]
            grads[odd * NC + which, :, cols] = pieces[s][fin : fin + fout, :]
            grads[(1 - odd) * NC + which, :, cols] = pieces[s][fin + fout :, :]
        part = jnp.dot(left, acts[:, cols], preferred_element_type=F32)
        out = jnp.zeros((32, 256), F32)
        for k in range(2 * NC):
            out += jnp.dot(rows_out[k], grads[k, :, cols], preferred_element_type=F32)
        rest = out - out.astype(BF16).astype(F32)
        for h in range(2):
            block = slice(h * 128, (h + 1) * 128)
            wide[pl.ds(h * height, height), :] = part[:, block]
            for i in range(4):
                wide[pl.ds(h * height + i * 16 + 14, NY, stride=64), :] = out[i * 8 : i * 8 + 8, block]
                wide[pl.ds(h * height + i * 16 + 15, NY, stride=64), :] = rest[i * 8 : i * 8 + 8, block]
            outs[s][:, :, block] = wide[h * height : (h + 1) * height].astype(BF16).reshape(CHIPS, 16, 128)
        results.append(pltpu.make_async_copy(outs[s], parts_ref.at[:, :, pl.ds(s * 256, 256)], sems.at[s]))
        results[-1].start()
    for result in results:
        result.wait()


def add_up(place, lens_ref, parts_ref, in_ref, out_ref, wide, narrow):
    x = place[0]
    halves = []
    for odd in range(2):
        mine = [zl * NY + y for zl in range(odd, NZL, 2) for y in range(NY)]
        part = parts_ref[mine[0]].astype(F32)
        for i in mine[1:]:
            part = part + parts_ref[i].astype(F32)
        halves.append(part)
    total = halves[0] + halves[1]
    for s in range(NX):
        source = lax.rem(x + s, NX)
        wide[:, pl.ds(pl.multiple_of(source * 256, 256), 256)] = total[:, s * 256 : (s + 1) * 256]
        for odd in range(2):
            for h in range(2):
                cols = slice((s * 2 + h) * 128, (s * 2 + h + 1) * 128)
                value = halves[odd][14:15, cols] + halves[odd][15:16, cols]
                narrow[pl.ds(odd * 8 + source * 2 + h, 1), :] = value
    wide[14:15, :128] = lens_ref[...]
    in_ref[...] = wide[...].astype(BF16)
    out_ref[...] = jnp.broadcast_to(narrow[...].astype(BF16)[None], out_ref.shape)


def documents(which, place, out_ref, *refs):
    pieces, (total_ref, rows_in, rows_out, sems) = refs[:NX], refs[NX:]
    x, zh = place[0], place[1]
    block = lax.rem(zh + which, NZH)
    copies = []
    for s in range(NX):
        copies.append(pltpu.make_async_copy(pieces[s], rows_in.at[lax.rem(x + s, NX)], sems.at[s]))
        copies[-1].start()
    rows_out[...] = out_ref[...].astype(F32).reshape(64 * 16, 128)
    position = lax.broadcasted_iota(jnp.int32, (1, 256), 1).astype(F32)
    for copy in copies:
        copy.wait()
    total = jnp.zeros((NX * 16, 64), F32)
    for g in range(NX):
        left = rows_in[:, :, g * 256 : (g + 1) * 256].astype(F32).reshape(NX * 16, 256)
        lens = rows_in[g, :, :128].astype(F32)[14:15, :4]
        right = []
        for h in range(2):
            cut = [
                rows_out[pl.ds(block * 512 + y * 128 + core * 16 + odd * 8 + g * 2 + h, 4, stride=32), :]
                for y in range(4)
                for core in range(NC)
                for odd in range(2)
            ]
            right.append(jnp.concatenate(cut, axis=0))
        right = jnp.concatenate(right, axis=1).astype(BF16)
        masked, start = [], jnp.zeros((1, 1), F32)
        for d in range(4):
            end = start + lens[:, d : d + 1]
            inside = (position >= start) & (position < end)
            masked.append(jnp.where(inside, left, 0.0).astype(BF16))
            start = end
        product = lax.dot_general(
            jnp.concatenate(masked, axis=0), right, (((1,), (1,)), ((), ())), preferred_element_type=F32
        )
        for d in range(4):
            one = product[d * 64 : (d + 1) * 64]
            total = total + one * one
    total = total * (1.0 / 2048.0)
    for i in range(NX):
        total_ref[i * 14 : (i + 1) * 14, :] = total[i * 16 : i * 16 + 14]


def body(acts, grads, basis_in, basis_out, doc_lengths):
    x, zh, core = lax.axis_index("x"), lax.axis_index("zh"), lax.axis_index("core")
    place = jnp.stack([x, zh, core, lax.rem(lax.axis_index("zl"), 2)]).astype(jnp.int32)
    tok, fin = acts.shape
    fout = grads.shape[1]
    rows = basis_in.shape[0] // NX
    tokens = NX * tok

    packed, grads_t = call(
        pack,
        (in_hbm((CHIPS, 16, NC * fin + fout)), jax.ShapeDtypeStruct((fout, tok), BF16)),
        [
            pltpu.VMEM((PARTS, 4 * rows, CHIPS // PARTS * NC * fin), BF16),
            pltpu.VMEM((8, CHIPS * NC * fout), BF16),
            pltpu.VMEM((tok, fout), BF16),
            pltpu.VMEM((fout, tok), BF16),
            pltpu.VMEM((PARTS, CHIPS // PARTS, 16, NC * fin + fout), BF16),
            pltpu.SemaphoreType.DMA((2 * PARTS + 4,)),
        ],
        (place, *map(from_hbm, (basis_in, basis_out, grads))),
        1 << 20,
        in_specs=[SMEM] + [ANY] * 3,
        out_spec=ANY,
    )
    packed = lax.all_to_all(packed, ("zl", "y"), split_axis=0, concat_axis=0, tiled=True)

    next_t = lax.ppermute(grads_t, "zl", [(0, 1), (1, 0), (2, 3), (3, 2)])
    payload = jnp.concatenate([acts.T, grads_t, next_t], axis=0)
    size = payload.shape[0] // 2
    right, left = from_offset(payload, "x", NX, 1), from_offset(payload, "x", NX, 3)
    far = [from_offset(right[:size], "x", NX, 1), from_offset(left[size:], "x", NX, 3)]
    own = [payload, right, jnp.concatenate(far, axis=0), left]
    other = [from_offset(v, "core", NC, 1) for v in own]

    parts = call(
        project,
        in_hbm((CHIPS, 16, tokens)),
        [
            pltpu.VMEM((NC * fin, tokens), BF16),
            pltpu.VMEM((2 * NC, fout, tokens), BF16),
            pltpu.VMEM((NY * 16, fout), F32),
            pltpu.VMEM((2 * CHIPS * 16, 128), F32),
            *[pltpu.VMEM((CHIPS, 16, 256), BF16)] * NX,
            pltpu.SemaphoreType.DMA((NX,)),
        ],
        (place, *map(in_vmem, (packed, *own, *other))),
        2 * 512 * 1024 * 1024,
        out_spec=ANY,
    )
    parts = lax.all_to_all(parts, ("zl", "y"), split_axis=0, concat_axis=0, tiled=True)
    lens = jnp.pad(doc_lengths.astype(F32), ((0, 0), (0, 124)))
    proj_in, proj_out = call(
        add_up,
        (jax.ShapeDtypeStruct((16, tokens), BF16), in_hbm((64, 16, 128))),
        [pltpu.VMEM((16, tokens), F32), pltpu.VMEM((16, 128), F32)],
        (place, lens, in_vmem(parts)),
        32 * 16 * 1024,
    )

    proj_out = lax.all_to_all(proj_out, ("zl", "y", "core"), split_axis=0, concat_axis=0, tiled=True)
    pieces = [proj_in] + [from_offset(proj_in, "x", NX, s) for s in range(1, NX)]
    operands = (place, in_vmem(proj_out), *pieces)
    totals = [
        call(
            functools.partial(documents, which),
            jax.ShapeDtypeStruct((NX * rows, 64), F32),
            [
                pltpu.VMEM((NX, 16, tokens), BF16),
                pltpu.VMEM((64 * 16, 128), F32),
                pltpu.SemaphoreType.DMA((NX,)),
            ],
            operands,
            2 * 4 * 256 * 256 * 64,
            in_specs=[SMEM, VMEM] + [ANY] * NX,
        )
        for which in range(NZH)
    ]
    return (totals[0] + from_offset(totals[1], "zh", NZH, 1)).T


def solution(mesh):
    fine = Mesh(mesh.devices.reshape(NX, NZH, NZL, NY, NC), ("x", "zh", "zl", "y", "core"))
    dp, mp = ("x", "zh"), ("zl", "y", "core")
    in_specs = (P(dp, mp), P(dp, mp), P(mp, None), P(mp, None), P(dp, None))
    return jax.shard_map(body, mesh=fine, in_specs=in_specs, out_specs=P(dp, mp), check_vma=False)
```

```python
import jax
import jax.numpy as jnp
from jax import lax
from jax.experimental import pallas as pl
from jax.experimental.pallas import tpu as pltpu
from jax.sharding import Mesh, PartitionSpec as P

NX, NZH, NZL, NY, NC = 4, 2, 4, 8, 2
CHIPS = NZL * NY
PARTS = 8
BF16, F32 = jnp.bfloat16, jnp.float32
SMEM = pl.BlockSpec(memory_space=pltpu.SMEM)
VMEM = pl.BlockSpec(memory_space=pltpu.VMEM)
ANY = pl.BlockSpec(memory_space=pl.ANY)


def from_offset(value, axis, size, offset):
    return lax.ppermute(value, axis, [((i + offset) % size, i) for i in range(size)])


def call(kernel, shapes, scratch, operands, flops, in_specs=None, out_spec=VMEM):
    size = sum(a.size * a.dtype.itemsize for a in operands)
    return pl.pallas_call(
        kernel,
        out_shape=shapes,
        in_specs=in_specs or [SMEM] + [VMEM] * (len(operands) - 1),
        out_specs=jax.tree.map(lambda _: out_spec, shapes),
        scratch_shapes=scratch,
        compiler_params=pltpu.CompilerParams(vmem_limit_bytes=40 << 20),
        cost_estimate=pl.CostEstimate(flops=flops, bytes_accessed=size, transcendentals=0),
    )(*operands)


def in_vmem(value):
    return pltpu.with_memory_space_constraint(value, pltpu.VMEM)


def from_hbm(value):
    return pltpu.with_memory_space_constraint(value, pltpu.HBM)


def in_hbm(shape):
    return pltpu.HBM(shape, BF16)


def pack(place, basis_ref, out_rows_ref, acts_ref, grads_ref, packed_ref, payload_ref, *scratch):
    basis, out_rows, grads, turned, packed, sems = scratch
    fin, fout = acts_ref.shape[0], grads_ref.shape[1]
    width, chips = NC * fin, CHIPS // PARTS
    loads = [
        pltpu.make_async_copy(out_rows_ref, out_rows, sems.at[0]),
        pltpu.make_async_copy(grads_ref, grads, sems.at[1]),
    ]
    for i in range(PARTS):
        cols = pl.ds(i * chips * width, chips * width)
        loads.append(pltpu.make_async_copy(basis_ref.at[:, cols], basis.at[i], sems.at[2 + i]))
    stores = [pltpu.make_async_copy(acts_ref, payload_ref.at[pl.ds(0, fin)], sems.at[2 + PARTS])]
    for copy in loads + stores:
        copy.start()
    loads[0].wait()
    for c in range(CHIPS):
        out = out_rows[:, c * NC * fout : (c + 1) * NC * fout].astype(F32)
        out = jnp.concatenate([out[:, :fout], out[:, fout:]], axis=0).astype(BF16)
        packed[c // chips, c % chips, :, width:] = out
    loads[1].wait()
    turned[...] = grads[...].astype(F32).T.astype(BF16)
    stores.append(pltpu.make_async_copy(turned, payload_ref.at[pl.ds(fin, fout)], sems.at[3 + PARTS]))
    stores[-1].start()
    for i in range(PARTS):
        loads[2 + i].wait()
        for x in range(NX):

            @pl.when(place[0] == x)
            def _():
                for c in range(chips):
                    rows = basis[i, :, c * width : (c + 1) * width].astype(F32)[x * 14 : (x + 1) * 14]
                    none = jnp.zeros((1, width), F32)
                    rows = jnp.concatenate([rows[:7], none, rows[7:], none], axis=0)
                    packed[i, c, :, :width] = rows.astype(BF16)

        there = packed_ref.at[pl.ds(i * chips, chips)]
        stores.append(pltpu.make_async_copy(packed.at[i], there, sems.at[4 + PARTS + i]))
        stores[-1].start()
    for store in stores:
        store.wait()


def project(place, packed_ref, *refs):
    own, other, parts_ref = refs[:NX], refs[NX : 2 * NX], refs[2 * NX]
    acts, grads, wide, low, *outs, sems = refs[2 * NX + 1 :]
    x, core = place[0], place[2]
    fin = acts.shape[0] // NC
    fout = grads.shape[1]
    tokens, height = acts.shape[1], CHIPS * 16
    left = packed_ref[:, :, : NC * fin].reshape(height, NC * fin)
    rows_out = packed_ref[pl.ds(x * 8, 8), :, NC * fin :].astype(F32).reshape(8, NC, 8, fout)
    rows_out = [rows_out[:, c].reshape(64, fout).astype(BF16) for c in range(NC)]
    results = []
    for s in range(NX):
        cols = slice(s * 256, (s + 1) * 256)
        for pieces, which in ((own, core), (other, 1 - core)):
            acts[pl.ds(pl.multiple_of(which * fin, 16), fin), cols] = pieces[s][:fin, :]
            grads[which, :, cols] = pieces[s][fin:, :]
        part = jnp.dot(left, acts[:, cols], preferred_element_type=F32)
        out = jnp.zeros((64, 256), F32)
        for c in range(NC):
            out += jnp.dot(rows_out[c], grads[c, :, cols], preferred_element_type=F32)
        rest = out - out.astype(BF16).astype(F32)
        for h in range(2):
            block = slice(h * 128, (h + 1) * 128)
            wide[pl.ds(h * height, height), :] = part[:, block]
            for half in range(NZH):
                mine = out[half * 32 : half * 32 + 32, block], rest[half * 32 : half * 32 + 32, block]
                wide[pl.ds(h * height + half * 8 + 7, CHIPS, stride=16), :] = mine[0]
                low[pl.ds(half * 8 + s * 2 + h, CHIPS, stride=16), :] = mine[1]
            for half in range(NZH):
                rows = wide[h * height : (h + 1) * height].reshape(CHIPS, NZH, 8, 128)[:, half]
                outs[s][half * CHIPS : (half + 1) * CHIPS, :, block] = rows.astype(BF16)
        results.append(pltpu.make_async_copy(outs[s], parts_ref.at[:, :, pl.ds(s * 256, 256)], sems.at[s]))
        results[-1].start()
    for half in range(NZH):
        rows = low[...].reshape(CHIPS, NZH, 8, 128)[:, half]
        outs[NX][half * CHIPS : (half + 1) * CHIPS] = rows.astype(BF16)
    results.append(pltpu.make_async_copy(outs[NX], parts_ref.at[:, :, pl.ds(tokens, 128)], sems.at[NX]))
    results[-1].start()
    for result in results:
        result.wait()


def add_in(place, lens_ref, parts_ref, in_ref, wide):
    x, tokens = place[0], wide.shape[1]
    for half in range(NZH):
        total = parts_ref[half * CHIPS, :, :tokens].astype(F32)
        for i in range(1, CHIPS):
            total = total + parts_ref[half * CHIPS + i, :, :tokens].astype(F32)
        for s in range(NX):
            there = pl.ds(pl.multiple_of(lax.rem(x + s, NX) * 256, 256), 256)
            wide[half * 8 : half * 8 + 8, there] = total[:, s * 256 : (s + 1) * 256]
    wide[7:8, :128] = lens_ref[...]
    in_ref[...] = wide[...].astype(BF16)


def add_out(place, parts_ref, _, out_ref, narrow):
    x, tokens = place[0], NX * 256
    for half in range(NZH):
        total = parts_ref[half * CHIPS].astype(F32)
        for i in range(1, CHIPS):
            total = total + parts_ref[half * CHIPS + i].astype(F32)
        for s in range(NX):
            for h in range(2):
                tile = s * 2 + h
                value = total[7:8, tile * 128 : (tile + 1) * 128] + total[tile : tile + 1, tokens:]
                narrow[pl.ds(half * 8 + lax.rem(x + s, NX) * 2 + h, 1), :] = value
    out_ref[...] = jnp.broadcast_to(narrow[...].astype(BF16)[None], out_ref.shape)


def documents(place, out_ref, *refs):
    pieces, (total_ref, rows_in, rows_out, sems) = refs[:NX], refs[NX:]
    x, zh = place[0], place[1]
    copies = []
    for s in range(NX):
        for half in range(NZH):
            there = rows_in.at[lax.rem(x + s, NX), lax.rem(half + zh, NZH)]
            copies.append(pltpu.make_async_copy(pieces[s].at[half], there, sems.at[s * NZH + half]))
            copies[-1].start()
    rows_out[...] = out_ref[...].astype(F32).reshape(64 * 16, 128)
    position = lax.broadcasted_iota(jnp.int32, (1, 256), 1).astype(F32)
    for copy in copies:
        copy.wait()
    total = jnp.zeros((64, 64), F32)
    for half in range(NZH):
        for g in range(NX):
            left = rows_in[:, :, :, g * 256 : (g + 1) * 256].astype(F32)
            left = left[:, :, half * 8 : half * 8 + 8].reshape(64, 256)
            lens = rows_in[g, half, :, :128].astype(F32)[7:8, :4]
            right = []
            for h in range(2):
                cut = [
                    rows_out[pl.ds((zl * 16 + core) * 16 + half * 8 + g * 2 + h, NY, stride=32), :]
                    for zl in range(NZL)
                    for core in range(NC)
                ]
                right.append(jnp.concatenate(cut, axis=0))
            right = jnp.concatenate(right, axis=1).astype(BF16)
            masked, start = [], jnp.zeros((1, 1), F32)
            for d in range(4):
                end = start + lens[:, d : d + 1]
                inside = (position >= start) & (position < end)
                masked.append(jnp.where(inside, left, 0.0).astype(BF16))
                start = end
            product = lax.dot_general(
                jnp.concatenate(masked, axis=0), right, (((1,), (1,)), ((), ())), preferred_element_type=F32
            )
            for d in range(4):
                one = product[d * 64 : (d + 1) * 64]
                total = total + one * one
    total = total * (1.0 / 2048.0)
    for i in range(NX * NZH):
        total_ref[i * 7 : (i + 1) * 7, :] = total[i * 8 : i * 8 + 7]


def body(acts, grads, basis_in, basis_out, doc_lengths):
    x, zh, core = lax.axis_index("x"), lax.axis_index("zh"), lax.axis_index("core")
    place = jnp.stack([x, zh, core]).astype(jnp.int32)
    tok, fin = acts.shape
    fout = grads.shape[1]
    rows = basis_in.shape[0] // NX
    tokens = NX * tok

    packed, payload = call(
        pack,
        (in_hbm((CHIPS, 16, NC * fin + fout)), jax.ShapeDtypeStruct((fin + fout, tok), BF16)),
        [
            pltpu.VMEM((PARTS, 4 * rows, CHIPS // PARTS * NC * fin), BF16),
            pltpu.VMEM((8, CHIPS * NC * fout), BF16),
            pltpu.VMEM((tok, fout), BF16),
            pltpu.VMEM((fout, tok), BF16),
            pltpu.VMEM((PARTS, CHIPS // PARTS, 16, NC * fin + fout), BF16),
            pltpu.SemaphoreType.DMA((2 * PARTS + 4,)),
        ],
        (place, *map(from_hbm, (basis_in, basis_out, acts.T, grads))),
        1 << 20,
        in_specs=[SMEM] + [ANY] * 4,
        out_spec=ANY,
    )
    packed = lax.all_to_all(packed, ("zl", "y"), split_axis=0, concat_axis=0, tiled=True)

    own = [payload] + [from_offset(payload, "x", NX, s) for s in range(1, NX)]
    other = [from_offset(v, "core", NC, 1) for v in own]

    parts = call(
        project,
        in_hbm((NZH * CHIPS, 8, tokens + 128)),
        [
            pltpu.VMEM((NC * fin, tokens), BF16),
            pltpu.VMEM((NC, fout, tokens), BF16),
            pltpu.VMEM((2 * CHIPS * 16, 128), F32),
            pltpu.VMEM((CHIPS * 16, 128), F32),
            *[pltpu.VMEM((NZH * CHIPS, 8, 256), BF16)] * NX,
            pltpu.VMEM((NZH * CHIPS, 8, 128), BF16),
            pltpu.SemaphoreType.DMA((5,)),
        ],
        (place, *map(in_vmem, (packed, *own, *other))),
        2 * 512 * 1024 * 1024,
        out_spec=ANY,
    )
    parts = lax.all_to_all(parts, ("zh", "zl", "y"), split_axis=0, concat_axis=0, tiled=True)
    parts = in_vmem(parts)
    lens = jnp.pad(doc_lengths.astype(F32), ((0, 0), (0, 124)))
    proj_in = call(
        add_in,
        jax.ShapeDtypeStruct((16, tokens), BF16),
        [pltpu.VMEM((16, tokens), F32)],
        (place, lens, parts),
        64 * 8 * 1024,
    )
    proj_out = call(
        add_out,
        in_hbm((64, 16, 128)),
        [pltpu.VMEM((16, 128), F32)],
        (place, parts, proj_in),
        64 * 8 * 1152,
        in_specs=[SMEM, VMEM, ANY],
    )

    pair = jnp.stack([proj_in, from_offset(proj_in, "zh", NZH, 1)])
    pieces = [pair] + [from_offset(pair, "x", NX, s) for s in range(1, NX)]
    proj_out = lax.all_to_all(proj_out, ("zl", "y", "core"), split_axis=0, concat_axis=0, tiled=True)
    total = call(
        documents,
        jax.ShapeDtypeStruct((NX * rows, 64), F32),
        [
            pltpu.VMEM((NX, NZH, 16, tokens), BF16),
            pltpu.VMEM((64 * 16, 128), F32),
            pltpu.SemaphoreType.DMA((NX * NZH,)),
        ],
        (place, in_vmem(proj_out), *pieces),
        2 * 8 * 256 * 256 * 64,
        in_specs=[SMEM, VMEM] + [ANY] * NX,
    )
    return total.T


def solution(mesh):
    fine = Mesh(mesh.devices.reshape(NX, NZH, NZL, NY, NC), ("x", "zh", "zl", "y", "core"))
    dp, mp = ("x", "zh"), ("zl", "y", "core")
    in_specs = (P(dp, mp), P(dp, mp), P(mp, None), P(mp, None), P(dp, None))
    return jax.shard_map(body, mesh=fine, in_specs=in_specs, out_specs=P(dp, mp), check_vma=False)
```

```python
import functools

import jax
import jax.numpy as jnp
from jax import lax
from jax.experimental import pallas as pl
from jax.experimental.pallas import tpu as pltpu
from jax.sharding import Mesh, PartitionSpec as P

NX, NZH, NZL, NY, NC = 4, 2, 4, 8, 2
CHIPS = NZL * NY
ORDER = [yb * 4 + ya for ya in range(4) for yb in range(2)]
BF16, F32 = jnp.bfloat16, jnp.float32
SMEM = pl.BlockSpec(memory_space=pltpu.SMEM)
VMEM = pl.BlockSpec(memory_space=pltpu.VMEM)
ANY = pl.BlockSpec(memory_space=pl.ANY)


def from_offset(value, axis, size, offset):
    return lax.ppermute(value, axis, [((i + offset) % size, i) for i in range(size)])


def call(kernel, shapes, scratch, operands, flops, in_specs=None, out_spec=VMEM):
    size = sum(a.size * a.dtype.itemsize for a in operands)
    return pl.pallas_call(
        kernel,
        out_shape=shapes,
        in_specs=in_specs or [SMEM] + [VMEM] * (len(operands) - 1),
        out_specs=jax.tree.map(lambda _: out_spec, shapes),
        scratch_shapes=scratch,
        compiler_params=pltpu.CompilerParams(vmem_limit_bytes=40 << 20),
        cost_estimate=pl.CostEstimate(flops=flops, bytes_accessed=size, transcendentals=0),
    )(*operands)


def in_vmem(value):
    return pltpu.with_memory_space_constraint(value, pltpu.VMEM)


def from_hbm(value):
    return pltpu.with_memory_space_constraint(value, pltpu.HBM)


def in_hbm(shape):
    return pltpu.HBM(shape, BF16)


def pack(place, basis_ref, out_rows_ref, acts_ref, grads_ref, packed_ref, payload_ref, *scratch):
    basis, out_rows, grads, turned, packed, sems = scratch
    fin, fout = acts_ref.shape[0], grads_ref.shape[1]
    width = NC * fin
    loads = [
        pltpu.make_async_copy(out_rows_ref, out_rows, sems.at[0]),
        pltpu.make_async_copy(grads_ref, grads, sems.at[1]),
    ]
    for zl in range(NZL):
        cols = pl.ds(zl * NY * width, NY * width)
        loads.append(pltpu.make_async_copy(basis_ref.at[:, cols], basis.at[zl], sems.at[2 + zl]))
    stores = [pltpu.make_async_copy(acts_ref, payload_ref.at[pl.ds(0, fin)], sems.at[2 + NZL])]
    for copy in loads + stores:
        copy.start()
    loads[0].wait()
    for zl in range(NZL):
        for i, y in enumerate(ORDER):
            first = (zl * NY + y) * NC * fout
            out = out_rows[:, first : first + NC * fout].astype(F32)
            packed[zl, i, :, width:] = jnp.concatenate([out[:, :fout], out[:, fout:]], axis=0).astype(BF16)
    loads[1].wait()
    turned[...] = grads[...].astype(F32).T.astype(BF16)
    stores.append(pltpu.make_async_copy(turned, payload_ref.at[pl.ds(fin, fout)], sems.at[3 + NZL]))
    stores[-1].start()
    for zl in range(NZL):
        loads[2 + zl].wait()
        for x in range(NX):

            @pl.when(place[0] == x)
            def _():
                for i, y in enumerate(ORDER):
                    rows = basis[zl, :, y * width : (y + 1) * width].astype(F32)[x * 14 : (x + 1) * 14]
                    rows = jnp.concatenate([rows, jnp.zeros((2, width), F32)], axis=0)
                    packed[zl, i, :, :width] = rows.astype(BF16)

        there = packed_ref.at[pl.ds(zl * NY, NY)]
        stores.append(pltpu.make_async_copy(packed.at[zl], there, sems.at[4 + NZL + zl]))
        stores[-1].start()
    for store in stores:
        store.wait()


def project(place, packed_ref, *refs):
    own, other, parts_ref = refs[:NX], refs[NX : 2 * NX], refs[2 * NX]
    acts, grads, wide, low, *outs, sems = refs[2 * NX + 1 :]
    x, core = place[0], place[2]
    fin = acts.shape[0] // NC
    fout = grads.shape[1]
    tokens, height = acts.shape[1], CHIPS * 16
    left = packed_ref[:, :, : NC * fin].reshape(height, NC * fin)
    rows_out = packed_ref[pl.ds(x * 8, 8), :, NC * fin :].astype(F32).reshape(8, NC, 8, fout)
    rows_out = [rows_out[:, c].reshape(64, fout).astype(BF16) for c in range(NC)]
    results = []
    for s in range(NX):
        cols = slice(s * 256, (s + 1) * 256)
        for pieces, which in ((own, core), (other, 1 - core)):
            acts[pl.ds(pl.multiple_of(which * fin, 16), fin), cols] = pieces[s][:fin, :]
            grads[which, :, cols] = pieces[s][fin:, :]
        part = jnp.dot(left, acts[:, cols], preferred_element_type=F32)
        out = jnp.zeros((64, 256), F32)
        for c in range(NC):
            out += jnp.dot(rows_out[c], grads[c, :, cols], preferred_element_type=F32)
        rest = out - out.astype(BF16).astype(F32)
        for h in range(2):
            block = slice(h * 128, (h + 1) * 128)
            wide[pl.ds(h * height, height), :] = part[:, block]
            for k, y in enumerate(ORDER):
                for yb in range(2):
                    mine = slice(k * 8 + yb * 4, k * 8 + yb * 4 + 4), block
                    first = ((y % 4) * NY + yb) * 16
                    wide[pl.ds(h * height + first + 14 + y // 4, 4, stride=32), :] = out[mine]
                    low[pl.ds(first + y // 4 * 8 + s * 2 + h, 4, stride=32), :] = rest[mine]
            outs[s][:, :, block] = wide[h * height : (h + 1) * height].astype(BF16).reshape(CHIPS, 16, 128)
        results.append(pltpu.make_async_copy(outs[s], parts_ref.at[:, :, pl.ds(s * 256, 256)], sems.at[s]))
        results[-1].start()
    outs[NX][...] = low[...].astype(BF16).reshape(CHIPS, 16, 128)
    results.append(pltpu.make_async_copy(outs[NX], parts_ref.at[:, :, pl.ds(tokens, 128)], sems.at[NX]))
    results[-1].start()
    for result in results:
        result.wait()


def add_up(place, lens_ref, parts_ref, in_ref, out_ref, wide, narrow):
    x = place[0]
    tokens = wide.shape[1]
    total = parts_ref[0].astype(F32)
    for i in range(1, CHIPS):
        total = total + parts_ref[i].astype(F32)
    for s in range(NX):
        source = lax.rem(x + s, NX)
        wide[:, pl.ds(pl.multiple_of(source * 256, 256), 256)] = total[:, s * 256 : (s + 1) * 256]
        for half in range(2):
            for h in range(2):
                col, row = s * 2 + h, half * 8 + s * 2 + h
                value = total[14 + half : 15 + half, col * 128 : (col + 1) * 128] + total[row : row + 1, tokens:]
                narrow[pl.ds(half * 8 + source * 2 + h, 1), :] = value
    wide[14:15, :128] = lens_ref[...]
    in_ref[...] = wide[...].astype(BF16)
    out_ref[...] = jnp.broadcast_to(narrow[...].astype(BF16)[None], out_ref.shape)


def documents(which, place, out_ref, *refs):
    pieces, (total_ref, rows_in, rows_out, sems) = refs[:NX], refs[NX:]
    x, zh = place[0], place[1]
    block = lax.rem(zh + which, NZH)
    copies = []
    for s in range(NX):
        copies.append(pltpu.make_async_copy(pieces[s], rows_in.at[lax.rem(x + s, NX)], sems.at[s]))
        copies[-1].start()
    rows_out[...] = out_ref[...].astype(F32).reshape(64 * 16, 128)
    position = lax.broadcasted_iota(jnp.int32, (1, 256), 1).astype(F32)
    for copy in copies:
        copy.wait()
    total = jnp.zeros((NX * 16, 64), F32)
    for g in range(NX):
        left = rows_in[:, :, g * 256 : (g + 1) * 256].astype(F32).reshape(NX * 16, 256)
        lens = rows_in[g, :, :128].astype(F32)[14:15, :4]
        right = []
        for h in range(2):
            cut = [
                rows_out[pl.ds((zl * 16 + core) * 16 + block * 8 + g * 2 + h, NY, stride=32), :]
                for zl in range(NZL)
                for core in range(NC)
            ]
            right.append(jnp.concatenate(cut, axis=0))
        right = jnp.concatenate(right, axis=1).astype(BF16)
        masked, start = [], jnp.zeros((1, 1), F32)
        for d in range(4):
            end = start + lens[:, d : d + 1]
            inside = (position >= start) & (position < end)
            masked.append(jnp.where(inside, left, 0.0).astype(BF16))
            start = end
        product = lax.dot_general(
            jnp.concatenate(masked, axis=0), right, (((1,), (1,)), ((), ())), preferred_element_type=F32
        )
        for d in range(4):
            one = product[d * 64 : (d + 1) * 64]
            total = total + one * one
    total = total * (1.0 / 2048.0)
    for i in range(NX):
        total_ref[i * 14 : (i + 1) * 14, :] = total[i * 16 : i * 16 + 14]


def body(acts, grads, basis_in, basis_out, doc_lengths):
    x, zh, core = lax.axis_index("x"), lax.axis_index("zh"), lax.axis_index("core")
    place = jnp.stack([x, zh, core]).astype(jnp.int32)
    tok, fin = acts.shape
    fout = grads.shape[1]
    rows = basis_in.shape[0] // NX
    tokens = NX * tok

    packed, payload = call(
        pack,
        (in_hbm((CHIPS, 16, NC * fin + fout)), jax.ShapeDtypeStruct((fin + fout, tok), BF16)),
        [
            pltpu.VMEM((NZL, 4 * rows, NY * NC * fin), BF16),
            pltpu.VMEM((8, CHIPS * NC * fout), BF16),
            pltpu.VMEM((tok, fout), BF16),
            pltpu.VMEM((fout, tok), BF16),
            pltpu.VMEM((NZL, NY, 16, NC * fin + fout), BF16),
            pltpu.SemaphoreType.DMA((2 * NZL + 4,)),
        ],
        (place, *map(from_hbm, (basis_in, basis_out, acts.T, grads))),
        1 << 20,
        in_specs=[SMEM] + [ANY] * 4,
        out_spec=ANY,
    )
    packed = lax.all_to_all(packed, ("zl", "ya", "yb"), split_axis=0, concat_axis=0, tiled=True)

    own = [payload] + [from_offset(payload, "x", NX, s) for s in range(1, NX)]
    other = [from_offset(v, "core", NC, 1) for v in own]

    parts = call(
        project,
        in_hbm((CHIPS, 16, tokens + 128)),
        [
            pltpu.VMEM((NC * fin, tokens), BF16),
            pltpu.VMEM((NC, fout, tokens), BF16),
            pltpu.VMEM((2 * CHIPS * 16, 128), F32),
            pltpu.VMEM((CHIPS * 16, 128), F32),
            *[pltpu.VMEM((CHIPS, 16, 256), BF16)] * NX,
            pltpu.VMEM((CHIPS, 16, 128), BF16),
            pltpu.SemaphoreType.DMA((5,)),
        ],
        (place, *map(in_vmem, (packed, *own, *other))),
        2 * 512 * 1024 * 1024,
        out_spec=ANY,
    )
    parts = lax.all_to_all(parts, ("zl", "ya", "yb"), split_axis=0, concat_axis=0, tiled=True)
    lens = jnp.pad(doc_lengths.astype(F32), ((0, 0), (0, 124)))
    proj_in, proj_out = call(
        add_up,
        (jax.ShapeDtypeStruct((16, tokens), BF16), in_hbm((64, 16, 128))),
        [pltpu.VMEM((16, tokens), F32), pltpu.VMEM((16, 128), F32)],
        (place, lens, in_vmem(parts)),
        32 * 16 * 1152,
    )

    proj_out = lax.all_to_all(proj_out, ("zl", "yb", "ya", "core"), split_axis=0, concat_axis=0, tiled=True)
    pieces = [proj_in] + [from_offset(proj_in, "x", NX, s) for s in range(1, NX)]
    operands = (place, in_vmem(proj_out), *pieces)
    totals = [
        call(
            functools.partial(documents, which),
            jax.ShapeDtypeStruct((NX * rows, 64), F32),
            [
                pltpu.VMEM((NX, 16, tokens), BF16),
                pltpu.VMEM((64 * 16, 128), F32),
                pltpu.SemaphoreType.DMA((NX,)),
            ],
            operands,
            2 * 4 * 256 * 256 * 64,
            in_specs=[SMEM, VMEM] + [ANY] * NX,
        )
        for which in range(NZH)
    ]
    return (totals[0] + from_offset(totals[1], "zh", NZH, 1)).T


def solution(mesh):
    fine = Mesh(mesh.devices.reshape(NX, NZH, NZL, 2, 4, NC), ("x", "zh", "zl", "yb", "ya", "core"))
    dp, mp = ("x", "zh"), ("zl", "yb", "ya", "core")
    in_specs = (P(dp, mp), P(dp, mp), P(mp, None), P(mp, None), P(dp, None))
    return jax.shard_map(body, mesh=fine, in_specs=in_specs, out_specs=P(dp, mp), check_vma=False)
```

```python
import jax
import jax.numpy as jnp
from jax import lax
from jax.experimental import pallas as pl
from jax.experimental.pallas import tpu as pltpu
from jax.sharding import Mesh, PartitionSpec as P

NX, NZH, NZL, NY, NC = 4, 2, 4, 8, 2
CHIPS = NZL * NY
PARTS = 8
BF16, F32 = jnp.bfloat16, jnp.float32
SMEM = pl.BlockSpec(memory_space=pltpu.SMEM)
VMEM = pl.BlockSpec(memory_space=pltpu.VMEM)
ANY = pl.BlockSpec(memory_space=pl.ANY)


def from_offset(value, axis, size, offset):
    return lax.ppermute(value, axis, [((i + offset) % size, i) for i in range(size)])


def call(kernel, shapes, scratch, operands, flops, in_specs=None, out_spec=VMEM):
    size = sum(a.size * a.dtype.itemsize for a in operands)
    return pl.pallas_call(
        kernel,
        out_shape=shapes,
        in_specs=in_specs or [SMEM] + [VMEM] * (len(operands) - 1),
        out_specs=jax.tree.map(lambda _: out_spec, shapes),
        scratch_shapes=scratch,
        compiler_params=pltpu.CompilerParams(vmem_limit_bytes=40 << 20),
        cost_estimate=pl.CostEstimate(flops=flops, bytes_accessed=size, transcendentals=0),
    )(*operands)


def in_vmem(value):
    return pltpu.with_memory_space_constraint(value, pltpu.VMEM)


def from_hbm(value):
    return pltpu.with_memory_space_constraint(value, pltpu.HBM)


def in_hbm(shape):
    return pltpu.HBM(shape, BF16)


def pack(place, basis_ref, out_rows_ref, acts_ref, grads_ref, packed_ref, payload_ref, *scratch):
    basis, out_rows, grads, turned, packed, sems = scratch
    fin, fout = acts_ref.shape[0], grads_ref.shape[1]
    width, chips = NC * fin, CHIPS // PARTS
    loads = [
        pltpu.make_async_copy(out_rows_ref, out_rows, sems.at[0]),
        pltpu.make_async_copy(grads_ref, grads, sems.at[1]),
    ]
    for i in range(PARTS):
        cols = pl.ds(i * chips * width, chips * width)
        loads.append(pltpu.make_async_copy(basis_ref.at[:, cols], basis.at[i], sems.at[2 + i]))
    stores = [pltpu.make_async_copy(acts_ref, payload_ref.at[pl.ds(0, fin)], sems.at[2 + PARTS])]
    for copy in loads + stores:
        copy.start()
    loads[0].wait()
    for c in range(CHIPS):
        out = out_rows[:, c * NC * fout : (c + 1) * NC * fout].astype(F32)
        out = jnp.concatenate([out[:, :fout], out[:, fout:]], axis=0).astype(BF16)
        packed[c // chips, c % chips, :, width:] = out
    loads[1].wait()
    turned[...] = grads[...].astype(F32).T.astype(BF16)
    stores.append(pltpu.make_async_copy(turned, payload_ref.at[pl.ds(fin, fout)], sems.at[3 + PARTS]))
    stores[-1].start()
    for i in range(PARTS):
        loads[2 + i].wait()
        for x in range(NX):

            @pl.when(place[0] == x)
            def _():
                for c in range(chips):
                    rows = basis[i, :, c * width : (c + 1) * width].astype(F32)[x * 14 : (x + 1) * 14]
                    rows = jnp.concatenate([rows, jnp.zeros((2, width), F32)], axis=0)
                    packed[i, c, :, :width] = rows.astype(BF16)

        there = packed_ref.at[pl.ds(i * chips, chips)]
        stores.append(pltpu.make_async_copy(packed.at[i], there, sems.at[4 + PARTS + i]))
        stores[-1].start()
    for store in stores:
        store.wait()


def project(place, packed_ref, *refs):
    own, other, parts_ref = refs[:NX], refs[NX : 2 * NX], refs[2 * NX]
    acts, grads, wide, low, *outs, sems = refs[2 * NX + 1 :]
    x, core = place[0], place[2]
    fin = acts.shape[0] // NC
    fout = grads.shape[1]
    tokens, height = acts.shape[1], CHIPS * 16
    left = packed_ref[:, :, : NC * fin].reshape(height, NC * fin)
    rows_out = packed_ref[pl.ds(x * 8, 8), :, NC * fin :].astype(F32).reshape(8, NC, 8, fout)
    rows_out = [rows_out[:, c].reshape(64, fout).astype(BF16) for c in range(NC)]
    results = []
    for s in range(NX):
        cols = slice(s * 256, (s + 1) * 256)
        for pieces, which in ((own, core), (other, 1 - core)):
            acts[pl.ds(pl.multiple_of(which * fin, 16), fin), cols] = pieces[s][:fin, :]
            grads[which, :, cols] = pieces[s][fin:, :]
        part = jnp.dot(left, acts[:, cols], preferred_element_type=F32)
        out = jnp.zeros((64, 256), F32)
        for c in range(NC):
            out += jnp.dot(rows_out[c], grads[c, :, cols], preferred_element_type=F32)
        rest = out - out.astype(BF16).astype(F32)
        for h in range(2):
            block = slice(h * 128, (h + 1) * 128)
            wide[pl.ds(h * height, height), :] = part[:, block]
            for half in range(2):
                wide[pl.ds(h * height + 14 + half, CHIPS, stride=16), :] = out[half * 32 : half * 32 + 32, block]
                low[pl.ds(half * 8 + s * 2 + h, CHIPS, stride=16), :] = rest[half * 32 : half * 32 + 32, block]
            outs[s][:, :, block] = wide[h * height : (h + 1) * height].astype(BF16).reshape(CHIPS, 16, 128)
        results.append(pltpu.make_async_copy(outs[s], parts_ref.at[:, :, pl.ds(s * 256, 256)], sems.at[s]))
        results[-1].start()
    outs[NX][...] = low[...].astype(BF16).reshape(CHIPS, 16, 128)
    results.append(pltpu.make_async_copy(outs[NX], parts_ref.at[:, :, pl.ds(tokens, 128)], sems.at[NX]))
    results[-1].start()
    for result in results:
        result.wait()


def add_up(place, lens_ref, parts_ref, in_ref, out_ref, wide, narrow):
    x = place[0]
    tokens = wide.shape[1]
    total = parts_ref[0].astype(F32)
    for i in range(1, CHIPS):
        total = total + parts_ref[i].astype(F32)
    for s in range(NX):
        source = lax.rem(x + s, NX)
        wide[:, pl.ds(pl.multiple_of(source * 256, 256), 256)] = total[:, s * 256 : (s + 1) * 256]
        for half in range(2):
            for h in range(2):
                col, row = s * 2 + h, half * 8 + s * 2 + h
                value = total[14 + half : 15 + half, col * 128 : (col + 1) * 128] + total[row : row + 1, tokens:]
                narrow[pl.ds(half * 8 + source * 2 + h, 1), :] = value
    wide[14:15, :128] = lens_ref[...]
    in_ref[...] = wide[...].astype(BF16)
    out_ref[...] = jnp.broadcast_to(narrow[...].astype(BF16)[None], out_ref.shape)


def documents(place, out_ref, in_ref, send_ref, keep_ref, rows_out):
    zh = place[1]
    rows_out[...] = out_ref[...].astype(F32).reshape(64 * 16, 128)
    position = lax.broadcasted_iota(jnp.int32, (1, 256), 1).astype(F32)
    total = jnp.zeros((NX * 16, 128), F32)
    for g in range(NX):
        left = in_ref[:, :, g * 256 : (g + 1) * 256].astype(F32).reshape(NX * 16, 256)
        lens = in_ref[g, :, :128].astype(F32)[14:15, :4]
        right = []
        for h in range(2):
            cut = [
                rows_out[pl.ds((zl * 16 + core) * 16 + block * 8 + g * 2 + h, NY, stride=32), :]
                for block in (1 - zh, zh)
                for zl in range(NZL)
                for core in range(NC)
            ]
            right.append(jnp.concatenate(cut, axis=0))
        right = jnp.concatenate(right, axis=1).astype(BF16)
        masked, start = [], jnp.zeros((1, 1), F32)
        for d in range(4):
            end = start + lens[:, d : d + 1]
            inside = (position >= start) & (position < end)
            masked.append(jnp.where(inside, left, 0.0).astype(BF16))
            start = end
        product = lax.dot_general(
            jnp.concatenate(masked, axis=0), right, (((1,), (1,)), ((), ())), preferred_element_type=F32
        )
        for d in range(4):
            one = product[d * 64 : (d + 1) * 64]
            total = total + one * one
    total = total * (1.0 / 2048.0)
    for i in range(NX):
        send_ref[i * 14 : (i + 1) * 14, :] = total[i * 16 : i * 16 + 14, :64]
        keep_ref[i * 14 : (i + 1) * 14, :] = total[i * 16 : i * 16 + 14, 64:]


def body(acts, grads, basis_in, basis_out, doc_lengths):
    x, zh, core = lax.axis_index("x"), lax.axis_index("zh"), lax.axis_index("core")
    place = jnp.stack([x, zh, core]).astype(jnp.int32)
    tok, fin = acts.shape
    fout = grads.shape[1]
    rows = basis_in.shape[0] // NX
    tokens = NX * tok

    packed, payload = call(
        pack,
        (in_hbm((CHIPS, 16, NC * fin + fout)), jax.ShapeDtypeStruct((fin + fout, tok), BF16)),
        [
            pltpu.VMEM((PARTS, 4 * rows, CHIPS // PARTS * NC * fin), BF16),
            pltpu.VMEM((8, CHIPS * NC * fout), BF16),
            pltpu.VMEM((tok, fout), BF16),
            pltpu.VMEM((fout, tok), BF16),
            pltpu.VMEM((PARTS, CHIPS // PARTS, 16, NC * fin + fout), BF16),
            pltpu.SemaphoreType.DMA((2 * PARTS + 4,)),
        ],
        (place, *map(from_hbm, (basis_in, basis_out, acts.T, grads))),
        1 << 20,
        in_specs=[SMEM] + [ANY] * 4,
        out_spec=ANY,
    )
    packed = lax.all_to_all(packed, ("zl", "y"), split_axis=0, concat_axis=0, tiled=True)

    own = [payload] + [from_offset(payload, "x", NX, s) for s in range(1, NX)]
    other = [from_offset(v, "core", NC, 1) for v in own]

    parts = call(
        project,
        in_hbm((CHIPS, 16, tokens + 128)),
        [
            pltpu.VMEM((NC * fin, tokens), BF16),
            pltpu.VMEM((NC, fout, tokens), BF16),
            pltpu.VMEM((2 * CHIPS * 16, 128), F32),
            pltpu.VMEM((CHIPS * 16, 128), F32),
            *[pltpu.VMEM((CHIPS, 16, 256), BF16)] * NX,
            pltpu.VMEM((CHIPS, 16, 128), BF16),
            pltpu.SemaphoreType.DMA((5,)),
        ],
        (place, *map(in_vmem, (packed, *own, *other))),
        2 * 512 * 1024 * 1024,
        out_spec=ANY,
    )
    parts = lax.all_to_all(parts, ("zl", "y"), split_axis=0, concat_axis=0, tiled=True)
    lens = jnp.pad(doc_lengths.astype(F32), ((0, 0), (0, 124)))
    proj_in, proj_out = call(
        add_up,
        (jax.ShapeDtypeStruct((16, tokens), BF16), in_hbm((64, 16, 128))),
        [pltpu.VMEM((16, tokens), F32), pltpu.VMEM((16, 128), F32)],
        (place, lens, in_vmem(parts)),
        32 * 16 * 1152,
    )

    proj_out = lax.all_to_all(proj_out, ("zl", "y", "core"), split_axis=0, concat_axis=0, tiled=True)
    proj_in = lax.all_gather(proj_in, "x")
    block = jax.ShapeDtypeStruct((NX * rows, 64), F32)
    send, keep = call(
        documents,
        (block, block),
        [pltpu.VMEM((64 * 16, 128), F32)],
        (place, *map(in_vmem, (proj_out, proj_in))),
        2 * 4 * 256 * 256 * 128,
    )
    both = lax.all_gather(send, "zh")
    return (keep + jnp.where(zh == 0, both[1], both[0])).T


def solution(mesh):
    fine = Mesh(mesh.devices.reshape(NX, NZH, NZL, NY, NC), ("x", "zh", "zl", "y", "core"))
    dp, mp = ("x", "zh"), ("zl", "y", "core")
    in_specs = (P(dp, mp), P(dp, mp), P(mp, None), P(mp, None), P(dp, None))
    return jax.shard_map(body, mesh=fine, in_specs=in_specs, out_specs=P(dp, mp), check_vma=False)
```

```python
import jax
import jax.numpy as jnp
from jax import lax
from jax.experimental import pallas as pl
from jax.experimental.pallas import tpu as pltpu
from jax.sharding import Mesh, PartitionSpec as P

NX, NZH, NZL, NY, NC = 4, 2, 4, 8, 2
CHIPS = NZL * NY
PARTS = 8
BF16, F32 = jnp.bfloat16, jnp.float32
SMEM = pl.BlockSpec(memory_space=pltpu.SMEM)
VMEM = pl.BlockSpec(memory_space=pltpu.VMEM)
ANY = pl.BlockSpec(memory_space=pl.ANY)


def from_offset(value, axis, size, offset):
    return lax.ppermute(value, axis, [((i + offset) % size, i) for i in range(size)])


def call(kernel, shapes, scratch, operands, flops, in_specs=None, out_spec=VMEM):
    size = sum(a.size * a.dtype.itemsize for a in operands)
    return pl.pallas_call(
        kernel,
        out_shape=shapes,
        in_specs=in_specs or [SMEM] + [VMEM] * (len(operands) - 1),
        out_specs=jax.tree.map(lambda _: out_spec, shapes),
        scratch_shapes=scratch,
        compiler_params=pltpu.CompilerParams(vmem_limit_bytes=40 << 20),
        cost_estimate=pl.CostEstimate(flops=flops, bytes_accessed=size, transcendentals=0),
    )(*operands)


def in_vmem(value):
    return pltpu.with_memory_space_constraint(value, pltpu.VMEM)


def from_hbm(value):
    return pltpu.with_memory_space_constraint(value, pltpu.HBM)


def in_hbm(shape):
    return pltpu.HBM(shape, BF16)


def pack(place, basis_ref, out_rows_ref, acts_ref, grads_ref, packed_ref, payload_ref, *scratch):
    basis, out_rows, grads, turned, packed, sems = scratch
    fin, fout = acts_ref.shape[0], grads_ref.shape[1]
    width, chips = NC * fin, CHIPS // PARTS
    loads = [
        pltpu.make_async_copy(out_rows_ref, out_rows, sems.at[0]),
        pltpu.make_async_copy(grads_ref, grads, sems.at[1]),
    ]
    for i in range(PARTS):
        cols = pl.ds(i * chips * width, chips * width)
        loads.append(pltpu.make_async_copy(basis_ref.at[:, cols], basis.at[i], sems.at[2 + i]))
    stores = [pltpu.make_async_copy(acts_ref, payload_ref.at[pl.ds(0, fin)], sems.at[2 + PARTS])]
    for copy in loads + stores:
        copy.start()
    loads[0].wait()
    for c in range(CHIPS):
        out = out_rows[:, c * NC * fout : (c + 1) * NC * fout].astype(F32)
        out = jnp.concatenate([out[:, :fout], out[:, fout:]], axis=0).astype(BF16)
        packed[c // chips, c % chips, :, width:] = out
    loads[1].wait()
    turned[...] = grads[...].astype(F32).T.astype(BF16)
    stores.append(pltpu.make_async_copy(turned, payload_ref.at[pl.ds(fin, fout)], sems.at[3 + PARTS]))
    stores[-1].start()
    for x in range(NX):

        @pl.when(place[0] == x)
        def _():
            for i in range(PARTS):
                loads[2 + i].wait()
                for c in range(chips):
                    rows = basis[i, :, c * width : (c + 1) * width].astype(F32)[x * 14 : (x + 1) * 14]
                    rows = jnp.concatenate([rows, jnp.zeros((2, width), F32)], axis=0)
                    packed[i, c, :, :width] = rows.astype(BF16)
                there = packed_ref.at[pl.ds(i * chips, chips)]
                pltpu.make_async_copy(packed.at[i], there, sems.at[4 + PARTS + i]).start()

    for i in range(PARTS):
        there = packed_ref.at[pl.ds(i * chips, chips)]
        stores.append(pltpu.make_async_copy(packed.at[i], there, sems.at[4 + PARTS + i]))
    for store in stores:
        store.wait()


def project(place, packed_ref, *refs):
    own, other, parts_ref = refs[:NX], refs[NX : 2 * NX], refs[2 * NX]
    acts, grads, wide, low, *outs, sems = refs[2 * NX + 1 :]
    x, core = place[0], place[2]
    fin = acts.shape[0] // NC
    fout = grads.shape[1]
    tokens, height = acts.shape[1], CHIPS * 16
    left = packed_ref[:, :, : NC * fin].reshape(height, NC * fin)
    rows_out = packed_ref[pl.ds(x * 8, 8), :, NC * fin :].astype(F32).reshape(8, NC, 8, fout)
    rows_out = [rows_out[:, c].reshape(64, fout).astype(BF16) for c in range(NC)]
    results = []
    for s in range(NX):
        cols = slice(s * 256, (s + 1) * 256)
        for pieces, which in ((own, core), (other, 1 - core)):
            acts[pl.ds(pl.multiple_of(which * fin, 16), fin), cols] = pieces[s][:fin, :]
            grads[which, :, cols] = pieces[s][fin:, :]
        part = jnp.dot(left, acts[:, cols], preferred_element_type=F32)
        out = jnp.zeros((64, 256), F32)
        for c in range(NC):
            out += jnp.dot(rows_out[c], grads[c, :, cols], preferred_element_type=F32)
        rest = out - out.astype(BF16).astype(F32)
        for h in range(2):
            block = slice(h * 128, (h + 1) * 128)
            wide[pl.ds(h * height, height), :] = part[:, block]
            for half in range(2):
                wide[pl.ds(h * height + 14 + half, CHIPS, stride=16), :] = out[half * 32 : half * 32 + 32, block]
                low[pl.ds(half * 8 + s * 2 + h, CHIPS, stride=16), :] = rest[half * 32 : half * 32 + 32, block]
            outs[s][:, :, block] = wide[h * height : (h + 1) * height].astype(BF16).reshape(CHIPS, 16, 128)
        results.append(pltpu.make_async_copy(outs[s], parts_ref.at[:, :, pl.ds(s * 256, 256)], sems.at[s]))
        results[-1].start()
    outs[NX][...] = low[...].astype(BF16).reshape(CHIPS, 16, 128)
    results.append(pltpu.make_async_copy(outs[NX], parts_ref.at[:, :, pl.ds(tokens, 128)], sems.at[NX]))
    results[-1].start()
    for result in results:
        result.wait()


def add_out(place, parts_ref, out_ref, narrow):
    x, tokens = place[0], NX * 256
    high = parts_ref[0, :, :tokens].astype(F32)[8:]
    low = parts_ref[0, :, tokens:].astype(F32)
    for i in range(1, CHIPS):
        high = high + parts_ref[i, :, :tokens].astype(F32)[8:]
        low = low + parts_ref[i, :, tokens:].astype(F32)
    for s in range(NX):
        source = lax.rem(x + s, NX)
        for half in range(2):
            for h in range(2):
                col, row = s * 2 + h, half * 8 + s * 2 + h
                value = high[6 + half : 7 + half, col * 128 : (col + 1) * 128] + low[row : row + 1]
                narrow[pl.ds(half * 8 + source * 2 + h, 1), :] = value
    out_ref[...] = jnp.broadcast_to(narrow[...].astype(BF16)[None], out_ref.shape)


def add_in(place, lens_ref, parts_ref, in_ref, wide):
    x, tokens = place[0], wide.shape[1]
    total = parts_ref[0, :, :tokens].astype(F32)
    for i in range(1, CHIPS):
        total = total + parts_ref[i, :, :tokens].astype(F32)
    for s in range(NX):
        there = pl.ds(pl.multiple_of(lax.rem(x + s, NX) * 256, 256), 256)
        wide[:, there] = total[:, s * 256 : (s + 1) * 256]
    wide[14:15, :128] = lens_ref[...]
    in_ref[...] = wide[...].astype(BF16)


def documents(place, out_ref, in_ref, send_ref, keep_ref, rows_out):
    zh = place[1]
    rows_out[...] = out_ref[...].astype(F32).reshape(64 * 16, 128)
    position = lax.broadcasted_iota(jnp.int32, (1, 256), 1).astype(F32)
    total = jnp.zeros((NX * 16, 128), F32)
    for g in range(NX):
        left = in_ref[:, :, g * 256 : (g + 1) * 256].astype(F32).reshape(NX * 16, 256)
        lens = in_ref[g, :, :128].astype(F32)[14:15, :4]
        right = []
        for h in range(2):
            cut = [
                rows_out[pl.ds((zl * 16 + core) * 16 + block * 8 + g * 2 + h, NY, stride=32), :]
                for block in (1 - zh, zh)
                for zl in range(NZL)
                for core in range(NC)
            ]
            right.append(jnp.concatenate(cut, axis=0))
        right = jnp.concatenate(right, axis=1).astype(BF16)
        masked, start = [], jnp.zeros((1, 1), F32)
        for d in range(4):
            end = start + lens[:, d : d + 1]
            inside = (position >= start) & (position < end)
            masked.append(jnp.where(inside, left, 0.0).astype(BF16))
            start = end
        product = lax.dot_general(
            jnp.concatenate(masked, axis=0), right, (((1,), (1,)), ((), ())), preferred_element_type=F32
        )
        for d in range(4):
            one = product[d * 64 : (d + 1) * 64]
            total = total + one * one
    total = total * (1.0 / 2048.0)
    for i in range(NX):
        send_ref[i * 14 : (i + 1) * 14, :] = total[i * 16 : i * 16 + 14, :64]
        keep_ref[i * 14 : (i + 1) * 14, :] = total[i * 16 : i * 16 + 14, 64:]


def body(acts, grads, basis_in, basis_out, doc_lengths):
    x, zh, core = lax.axis_index("x"), lax.axis_index("zh"), lax.axis_index("core")
    place = jnp.stack([x, zh, core]).astype(jnp.int32)
    tok, fin = acts.shape
    fout = grads.shape[1]
    rows = basis_in.shape[0] // NX
    tokens = NX * tok

    packed, payload = call(
        pack,
        (in_hbm((CHIPS, 16, NC * fin + fout)), jax.ShapeDtypeStruct((fin + fout, tok), BF16)),
        [
            pltpu.VMEM((PARTS, 4 * rows, CHIPS // PARTS * NC * fin), BF16),
            pltpu.VMEM((8, CHIPS * NC * fout), BF16),
            pltpu.VMEM((tok, fout), BF16),
            pltpu.VMEM((fout, tok), BF16),
            pltpu.VMEM((PARTS, CHIPS // PARTS, 16, NC * fin + fout), BF16),
            pltpu.SemaphoreType.DMA((2 * PARTS + 4,)),
        ],
        (place, *map(from_hbm, (basis_in, basis_out, acts.T, grads))),
        1 << 20,
        in_specs=[SMEM] + [ANY] * 4,
        out_spec=ANY,
    )
    packed = lax.all_to_all(packed, ("zl", "y"), split_axis=0, concat_axis=0, tiled=True)

    own = [payload] + [from_offset(payload, "x", NX, s) for s in range(1, NX)]
    other = [from_offset(v, "core", NC, 1) for v in own]

    parts = call(
        project,
        in_hbm((CHIPS, 16, tokens + 128)),
        [
            pltpu.VMEM((NC * fin, tokens), BF16),
            pltpu.VMEM((NC, fout, tokens), BF16),
            pltpu.VMEM((2 * CHIPS * 16, 128), F32),
            pltpu.VMEM((CHIPS * 16, 128), F32),
            *[pltpu.VMEM((CHIPS, 16, 256), BF16)] * NX,
            pltpu.VMEM((CHIPS, 16, 128), BF16),
            pltpu.SemaphoreType.DMA((5,)),
        ],
        (place, *map(in_vmem, (packed, *own, *other))),
        2 * 512 * 1024 * 1024,
        out_spec=ANY,
    )
    parts = lax.all_to_all(parts, ("zl", "y"), split_axis=0, concat_axis=0, tiled=True)
    lens = jnp.pad(doc_lengths.astype(F32), ((0, 0), (0, 124)))
    parts = in_vmem(parts)
    proj_out = call(add_out, in_hbm((64, 16, 128)), [pltpu.VMEM((16, 128), F32)], (place, parts), 32 * 16 * 640)
    proj_in = call(
        add_in,
        jax.ShapeDtypeStruct((16, tokens), BF16),
        [pltpu.VMEM((16, tokens), F32)],
        (place, lens, parts),
        32 * 16 * 1024,
    )

    proj_out = lax.all_to_all(proj_out, ("zl", "y", "core"), split_axis=0, concat_axis=0, tiled=True)
    proj_in = lax.all_gather(proj_in, "x")
    block = jax.ShapeDtypeStruct((NX * rows, 64), F32)
    send, keep = call(
        documents,
        (block, block),
        [pltpu.VMEM((64 * 16, 128), F32)],
        (place, *map(in_vmem, (proj_out, proj_in))),
        2 * 4 * 256 * 256 * 128,
    )
    both = lax.all_gather(send, "zh")
    return (keep + jnp.where(zh == 0, both[1], both[0])).T


def solution(mesh):
    fine = Mesh(mesh.devices.reshape(NX, NZH, NZL, NY, NC), ("x", "zh", "zl", "y", "core"))
    dp, mp = ("x", "zh"), ("zl", "y", "core")
    in_specs = (P(dp, mp), P(dp, mp), P(mp, None), P(mp, None), P(dp, None))
    return jax.shard_map(body, mesh=fine, in_specs=in_specs, out_specs=P(dp, mp), check_vma=False)
```

```python
import jax
import jax.numpy as jnp
from jax import lax
from jax.experimental import pallas as pl
from jax.experimental.pallas import tpu as pltpu
from jax.sharding import Mesh, PartitionSpec as P

NX, NZH, NZL, NY, NC = 4, 2, 4, 8, 2
CHIPS = NZL * NY
PARTS = 8
BF16, F32 = jnp.bfloat16, jnp.float32
SMEM = pl.BlockSpec(memory_space=pltpu.SMEM)
VMEM = pl.BlockSpec(memory_space=pltpu.VMEM)
ANY = pl.BlockSpec(memory_space=pl.ANY)


def from_offset(value, axis, size, offset):
    return lax.ppermute(value, axis, [((i + offset) % size, i) for i in range(size)])


def call(kernel, shapes, scratch, operands, flops, in_specs=None, out_spec=VMEM):
    size = sum(a.size * a.dtype.itemsize for a in operands)
    return pl.pallas_call(
        kernel,
        out_shape=shapes,
        in_specs=in_specs or [SMEM] + [VMEM] * (len(operands) - 1),
        out_specs=jax.tree.map(lambda _: out_spec, shapes),
        scratch_shapes=scratch,
        compiler_params=pltpu.CompilerParams(vmem_limit_bytes=40 << 20),
        cost_estimate=pl.CostEstimate(flops=flops, bytes_accessed=size, transcendentals=0),
    )(*operands)


def in_vmem(value):
    return pltpu.with_memory_space_constraint(value, pltpu.VMEM)


def from_hbm(value):
    return pltpu.with_memory_space_constraint(value, pltpu.HBM)


def in_hbm(shape):
    return pltpu.HBM(shape, BF16)


def pack(place, basis_ref, out_rows_ref, acts_ref, grads_ref, packed_ref, payload_ref, *scratch):
    basis, out_rows, grads, turned, packed, sems = scratch
    fin, fout = acts_ref.shape[0], grads_ref.shape[1]
    width, chips = NC * fin, CHIPS // PARTS
    loads = [
        pltpu.make_async_copy(out_rows_ref, out_rows, sems.at[0]),
        pltpu.make_async_copy(grads_ref, grads, sems.at[1]),
    ]
    for i in range(PARTS):
        cols = pl.ds(i * chips * width, chips * width)
        loads.append(pltpu.make_async_copy(basis_ref.at[:, cols], basis.at[i], sems.at[2 + i]))
    stores = [pltpu.make_async_copy(acts_ref, payload_ref.at[pl.ds(0, fin)], sems.at[2 + PARTS])]
    for copy in loads + stores:
        copy.start()
    loads[0].wait()
    for c in range(CHIPS):
        out = out_rows[:, c * NC * fout : (c + 1) * NC * fout].astype(F32)
        out = jnp.concatenate([out[:, :fout], out[:, fout:]], axis=0).astype(BF16)
        packed[c // chips, c % chips, :, width:] = out
    loads[1].wait()
    turned[...] = grads[...].astype(F32).T.astype(BF16)
    stores.append(pltpu.make_async_copy(turned, payload_ref.at[pl.ds(fin, fout)], sems.at[3 + PARTS]))
    stores[-1].start()
    for i in range(PARTS):
        loads[2 + i].wait()
        for x in range(NX):

            @pl.when(place[0] == x)
            def _():
                for c in range(chips):
                    rows = basis[i, :, c * width : (c + 1) * width].astype(F32)[x * 14 : (x + 1) * 14]
                    rows = jnp.concatenate([rows, jnp.zeros((2, width), F32)], axis=0)
                    packed[i, c, :, :width] = rows.astype(BF16)

        there = packed_ref.at[pl.ds(i * chips, chips)]
        stores.append(pltpu.make_async_copy(packed.at[i], there, sems.at[4 + PARTS + i]))
        stores[-1].start()
    for store in stores:
        store.wait()


def project(place, packed_ref, *refs):
    own, other, parts_ref = refs[:NX], refs[NX : 2 * NX], refs[2 * NX]
    acts, grads, wide, low, *outs, sems = refs[2 * NX + 1 :]
    x, core = place[0], place[2]
    fin = acts.shape[0] // NC
    fout = grads.shape[1]
    tokens, height = acts.shape[1], CHIPS * 16
    left = packed_ref[:, :, : NC * fin].reshape(height, NC * fin)
    rows_out = packed_ref[pl.ds(x * 8, 8), :, NC * fin :].astype(F32).reshape(8, NC, 8, fout)
    rows_out = [rows_out[:, c].reshape(64, fout).astype(BF16) for c in range(NC)]
    results = []
    for s in range(NX):
        cols = slice(s * 256, (s + 1) * 256)
        for pieces, which in ((own, core), (other, 1 - core)):
            acts[pl.ds(pl.multiple_of(which * fin, 16), fin), cols] = pieces[s][:fin, :]
            grads[which, :, cols] = pieces[s][fin:, :]
        part = jnp.dot(left, acts[:, cols], preferred_element_type=F32)
        out = jnp.zeros((64, 256), F32)
        for c in range(NC):
            out += jnp.dot(rows_out[c], grads[c, :, cols], preferred_element_type=F32)
        rest = out - out.astype(BF16).astype(F32)
        for h in range(2):
            block = slice(h * 128, (h + 1) * 128)
            wide[pl.ds(h * height, height), :] = part[:, block]
            for half in range(2):
                wide[pl.ds(h * height + 14 + half, CHIPS, stride=16), :] = out[half * 32 : half * 32 + 32, block]
                low[pl.ds(half * 8 + s * 2 + h, CHIPS, stride=16), :] = rest[half * 32 : half * 32 + 32, block]
            outs[s][:, :, block] = wide[h * height : (h + 1) * height].astype(BF16).reshape(CHIPS, 16, 128)
        results.append(pltpu.make_async_copy(outs[s], parts_ref.at[:, :, pl.ds(s * 256, 256)], sems.at[s]))
        results[-1].start()
    outs[NX][...] = low[...].astype(BF16).reshape(CHIPS, 16, 128)
    results.append(pltpu.make_async_copy(outs[NX], parts_ref.at[:, :, pl.ds(tokens, 128)], sems.at[NX]))
    results[-1].start()
    for result in results:
        result.wait()


def add_up(place, lens_ref, parts_ref, in_ref, out_ref, wide, narrow):
    x = place[0]
    tokens = wide.shape[1]
    total = parts_ref[0].astype(F32)
    for i in range(1, CHIPS):
        total = total + parts_ref[i].astype(F32)
    for s in range(NX):
        source = lax.rem(x + s, NX)
        wide[:, pl.ds(pl.multiple_of(source * 256, 256), 256)] = total[:, s * 256 : (s + 1) * 256]
        for half in range(2):
            for h in range(2):
                col, row = s * 2 + h, half * 8 + s * 2 + h
                value = total[14 + half : 15 + half, col * 128 : (col + 1) * 128] + total[row : row + 1, tokens:]
                narrow[pl.ds(half * 8 + source * 2 + h, 1), :] = value
    wide[14:15, :128] = lens_ref[...]
    in_ref[...] = wide[...].astype(BF16)
    out_ref[...] = jnp.broadcast_to(narrow[...].astype(BF16)[None], out_ref.shape)


def documents(place, out_ref, in_ref, both_ref, rows_out):
    rows_out[...] = out_ref[...].astype(F32).reshape(64 * 16, 128)
    position = lax.broadcasted_iota(jnp.int32, (1, 256), 1).astype(F32)
    total = jnp.zeros((NX * 16, 128), F32)
    for g in range(NX):
        left = in_ref[:, :, g * 256 : (g + 1) * 256].astype(F32).reshape(NX * 16, 256)
        lens = in_ref[g, :, :128].astype(F32)[14:15, :4]
        right = []
        for h in range(2):
            cut = [
                rows_out[pl.ds((zl * 16 + core) * 16 + block * 8 + g * 2 + h, NY, stride=32), :]
                for block in range(NZH)
                for zl in range(NZL)
                for core in range(NC)
            ]
            right.append(jnp.concatenate(cut, axis=0))
        right = jnp.concatenate(right, axis=1).astype(BF16)
        masked, start = [], jnp.zeros((1, 1), F32)
        for d in range(4):
            end = start + lens[:, d : d + 1]
            inside = (position >= start) & (position < end)
            masked.append(jnp.where(inside, left, 0.0).astype(BF16))
            start = end
        product = lax.dot_general(
            jnp.concatenate(masked, axis=0), right, (((1,), (1,)), ((), ())), preferred_element_type=F32
        )
        for d in range(4):
            one = product[d * 64 : (d + 1) * 64]
            total = total + one * one
    total = total * (1.0 / 2048.0)
    for i in range(NX):
        for block in range(NZH):
            both_ref[block, i * 14 : (i + 1) * 14, :] = total[i * 16 : i * 16 + 14, block * 64 : (block + 1) * 64]


def body(acts, grads, basis_in, basis_out, doc_lengths):
    x, zh, core = lax.axis_index("x"), lax.axis_index("zh"), lax.axis_index("core")
    place = jnp.stack([x, zh, core]).astype(jnp.int32)
    tok, fin = acts.shape
    fout = grads.shape[1]
    rows = basis_in.shape[0] // NX
    tokens = NX * tok

    packed, payload = call(
        pack,
        (in_hbm((CHIPS, 16, NC * fin + fout)), jax.ShapeDtypeStruct((fin + fout, tok), BF16)),
        [
            pltpu.VMEM((PARTS, 4 * rows, CHIPS // PARTS * NC * fin), BF16),
            pltpu.VMEM((8, CHIPS * NC * fout), BF16),
            pltpu.VMEM((tok, fout), BF16),
            pltpu.VMEM((fout, tok), BF16),
            pltpu.VMEM((PARTS, CHIPS // PARTS, 16, NC * fin + fout), BF16),
            pltpu.SemaphoreType.DMA((2 * PARTS + 4,)),
        ],
        (place, *map(from_hbm, (basis_in, basis_out, acts.T, grads))),
        1 << 20,
        in_specs=[SMEM] + [ANY] * 4,
        out_spec=ANY,
    )
    packed = lax.all_to_all(packed, ("zl", "y"), split_axis=0, concat_axis=0, tiled=True)

    own = [payload] + [from_offset(payload, "x", NX, s) for s in range(1, NX)]
    other = [from_offset(v, "core", NC, 1) for v in own]

    parts = call(
        project,
        in_hbm((CHIPS, 16, tokens + 128)),
        [
            pltpu.VMEM((NC * fin, tokens), BF16),
            pltpu.VMEM((NC, fout, tokens), BF16),
            pltpu.VMEM((2 * CHIPS * 16, 128), F32),
            pltpu.VMEM((CHIPS * 16, 128), F32),
            *[pltpu.VMEM((CHIPS, 16, 256), BF16)] * NX,
            pltpu.VMEM((CHIPS, 16, 128), BF16),
            pltpu.SemaphoreType.DMA((5,)),
        ],
        (place, *map(in_vmem, (packed, *own, *other))),
        2 * 512 * 1024 * 1024,
        out_spec=ANY,
    )
    parts = lax.all_to_all(parts, ("zl", "y"), split_axis=0, concat_axis=0, tiled=True)
    lens = jnp.pad(doc_lengths.astype(F32), ((0, 0), (0, 124)))
    proj_in, proj_out = call(
        add_up,
        (jax.ShapeDtypeStruct((16, tokens), BF16), in_hbm((64, 16, 128))),
        [pltpu.VMEM((16, tokens), F32), pltpu.VMEM((16, 128), F32)],
        (place, lens, in_vmem(parts)),
        32 * 16 * 1152,
    )

    proj_out = lax.all_to_all(proj_out, ("zl", "y", "core"), split_axis=0, concat_axis=0, tiled=True)
    proj_in = lax.all_gather(proj_in, "x")
    both = call(
        documents,
        jax.ShapeDtypeStruct((NZH, NX * rows, 64), F32),
        [pltpu.VMEM((64 * 16, 128), F32)],
        (place, *map(in_vmem, (proj_out, proj_in))),
        2 * 4 * 256 * 256 * 128,
    )
    both = lax.all_to_all(both, "zh", split_axis=0, concat_axis=0, tiled=True)
    return (both[0] + both[1]).T


def solution(mesh):
    fine = Mesh(mesh.devices.reshape(NX, NZH, NZL, NY, NC), ("x", "zh", "zl", "y", "core"))
    dp, mp = ("x", "zh"), ("zl", "y", "core")
    in_specs = (P(dp, mp), P(dp, mp), P(mp, None), P(mp, None), P(dp, None))
    return jax.shard_map(body, mesh=fine, in_specs=in_specs, out_specs=P(dp, mp), check_vma=False)
```

```python
import jax
import jax.numpy as jnp
from jax import lax
from jax.experimental import pallas as pl
from jax.experimental.pallas import tpu as pltpu
from jax.sharding import Mesh, PartitionSpec as P

NX, NZH, NZL, NY, NC = 4, 2, 4, 8, 2
CHIPS = NZL * NY
PARTS = 8
BF16, F32 = jnp.bfloat16, jnp.float32
SMEM = pl.BlockSpec(memory_space=pltpu.SMEM)
VMEM = pl.BlockSpec(memory_space=pltpu.VMEM)
ANY = pl.BlockSpec(memory_space=pl.ANY)


def from_offset(value, axis, size, offset):
    return lax.ppermute(value, axis, [((i + offset) % size, i) for i in range(size)])


def call(kernel, shapes, scratch, operands, flops, in_specs=None, out_spec=VMEM):
    size = sum(a.size * a.dtype.itemsize for a in operands)
    return pl.pallas_call(
        kernel,
        out_shape=shapes,
        in_specs=in_specs or [SMEM] + [VMEM] * (len(operands) - 1),
        out_specs=jax.tree.map(lambda _: out_spec, shapes),
        scratch_shapes=scratch,
        compiler_params=pltpu.CompilerParams(vmem_limit_bytes=40 << 20),
        cost_estimate=pl.CostEstimate(flops=flops, bytes_accessed=size, transcendentals=0),
    )(*operands)


def in_vmem(value):
    return pltpu.with_memory_space_constraint(value, pltpu.VMEM)


def from_hbm(value):
    return pltpu.with_memory_space_constraint(value, pltpu.HBM)


def in_hbm(shape):
    return pltpu.HBM(shape, BF16)


def pack(place, basis_ref, out_rows_ref, acts_ref, grads_ref, packed_ref, payload_ref, *scratch):
    basis, out_rows, grads, turned, packed, sems = scratch
    fin, fout = acts_ref.shape[0], grads_ref.shape[1]
    width, chips = NC * fin, CHIPS // PARTS
    loads = [
        pltpu.make_async_copy(out_rows_ref, out_rows, sems.at[0]),
        pltpu.make_async_copy(grads_ref, grads, sems.at[1]),
    ]
    for i in range(PARTS):
        cols = pl.ds(i * chips * width, chips * width)
        loads.append(pltpu.make_async_copy(basis_ref.at[:, cols], basis.at[i], sems.at[2 + i]))
    stores = [pltpu.make_async_copy(acts_ref, payload_ref.at[pl.ds(0, fin)], sems.at[2 + PARTS])]
    for copy in loads + stores:
        copy.start()
    loads[0].wait()
    for c in range(CHIPS):
        out = out_rows[:, c * NC * fout : (c + 1) * NC * fout].astype(F32)
        out = jnp.concatenate([out[:, :fout], out[:, fout:]], axis=0).astype(BF16)
        packed[c // chips, c % chips, :, width:] = out
    loads[1].wait()
    turned[...] = grads[...].astype(F32).T.astype(BF16)
    stores.append(pltpu.make_async_copy(turned, payload_ref.at[pl.ds(fin, fout)], sems.at[3 + PARTS]))
    stores[-1].start()
    for i in range(PARTS):
        loads[2 + i].wait()
        for x in range(NX):

            @pl.when(place[0] == x)
            def _():
                for c in range(chips):
                    rows = basis[i, :, c * width : (c + 1) * width].astype(F32)[x * 14 : (x + 1) * 14]
                    rows = jnp.concatenate([rows, jnp.zeros((2, width), F32)], axis=0)
                    packed[i, c, :, :width] = rows.astype(BF16)

        there = packed_ref.at[pl.ds(i * chips, chips)]
        stores.append(pltpu.make_async_copy(packed.at[i], there, sems.at[4 + PARTS + i]))
        stores[-1].start()
    for store in stores:
        store.wait()


def project(place, packed_ref, *refs):
    own, other, parts_ref = refs[:NX], refs[NX : 2 * NX], refs[2 * NX]
    wide, low, *outs, sems = refs[2 * NX + 1 :]
    x, core = place[0], place[2]
    fout = parts_ref.shape[2] - NX * 256
    fin = own[0].shape[0] - fout
    tokens, height = NX * 256, CHIPS * 16

    def by_core(halves):
        return jnp.where(core == 0, halves[0], halves[1]), jnp.where(core == 0, halves[1], halves[0])

    left = packed_ref[:, :, : NC * fin].reshape(height, NC * fin)
    left = by_core([left[:, c * fin : (c + 1) * fin] for c in range(NC)])
    rows_out = packed_ref[pl.ds(x * 8, 8), :, NC * fin :].astype(F32).reshape(8, NC, 8, fout)
    rows_out = by_core([rows_out[:, c].reshape(64, fout).astype(BF16) for c in range(NC)])
    results = []
    for s in range(NX):
        part, out = 0.0, 0.0
        for k, pieces in enumerate((own, other)):
            part += jnp.dot(left[k], pieces[s][:fin, :], preferred_element_type=F32)
            out += jnp.dot(rows_out[k], pieces[s][fin:, :], preferred_element_type=F32)
        rest = out - out.astype(BF16).astype(F32)
        for h in range(2):
            block = slice(h * 128, (h + 1) * 128)
            wide[pl.ds(h * height, height), :] = part[:, block]
            for half in range(2):
                wide[pl.ds(h * height + 14 + half, CHIPS, stride=16), :] = out[half * 32 : half * 32 + 32, block]
                low[pl.ds(half * 8 + s * 2 + h, CHIPS, stride=16), :] = rest[half * 32 : half * 32 + 32, block]
            outs[s][:, :, block] = wide[h * height : (h + 1) * height].astype(BF16).reshape(CHIPS, 16, 128)
        results.append(pltpu.make_async_copy(outs[s], parts_ref.at[:, :, pl.ds(s * 256, 256)], sems.at[s]))
        results[-1].start()
    outs[NX][...] = low[...].astype(BF16).reshape(CHIPS, 16, 128)
    results.append(pltpu.make_async_copy(outs[NX], parts_ref.at[:, :, pl.ds(tokens, 128)], sems.at[NX]))
    results[-1].start()
    for result in results:
        result.wait()


def add_up(place, lens_ref, parts_ref, in_ref, out_ref, wide, narrow):
    x = place[0]
    tokens = wide.shape[1]
    total = parts_ref[0].astype(F32)
    for i in range(1, CHIPS):
        total = total + parts_ref[i].astype(F32)
    for s in range(NX):
        source = lax.rem(x + s, NX)
        wide[:, pl.ds(pl.multiple_of(source * 256, 256), 256)] = total[:, s * 256 : (s + 1) * 256]
        for half in range(2):
            for h in range(2):
                col, row = s * 2 + h, half * 8 + s * 2 + h
                value = total[14 + half : 15 + half, col * 128 : (col + 1) * 128] + total[row : row + 1, tokens:]
                narrow[pl.ds(half * 8 + source * 2 + h, 1), :] = value
    wide[14:15, :128] = lens_ref[...]
    in_ref[...] = wide[...].astype(BF16)
    out_ref[...] = jnp.broadcast_to(narrow[...].astype(BF16)[None], out_ref.shape)


def documents(place, out_ref, in_ref, send_ref, keep_ref, rows_out):
    zh = place[1]
    rows_out[...] = out_ref[...].astype(F32).reshape(64 * 16, 128)
    position = lax.broadcasted_iota(jnp.int32, (1, 256), 1).astype(F32)
    total = jnp.zeros((NX * 16, 128), F32)
    for g in range(NX):
        left = in_ref[:, :, g * 256 : (g + 1) * 256].astype(F32).reshape(NX * 16, 256)
        lens = in_ref[g, :, :128].astype(F32)[14:15, :4]
        right = []
        for h in range(2):
            cut = [
                rows_out[pl.ds((zl * 16 + core) * 16 + block * 8 + g * 2 + h, NY, stride=32), :]
                for block in (1 - zh, zh)
                for zl in range(NZL)
                for core in range(NC)
            ]
            right.append(jnp.concatenate(cut, axis=0))
        right = jnp.concatenate(right, axis=1).astype(BF16)
        masked, start = [], jnp.zeros((1, 1), F32)
        for d in range(4):
            end = start + lens[:, d : d + 1]
            inside = (position >= start) & (position < end)
            masked.append(jnp.where(inside, left, 0.0).astype(BF16))
            start = end
        product = lax.dot_general(
            jnp.concatenate(masked, axis=0), right, (((1,), (1,)), ((), ())), preferred_element_type=F32
        )
        for d in range(4):
            one = product[d * 64 : (d + 1) * 64]
            total = total + one * one
    total = total * (1.0 / 2048.0)
    for i in range(NX):
        send_ref[i * 14 : (i + 1) * 14, :] = total[i * 16 : i * 16 + 14, :64]
        keep_ref[i * 14 : (i + 1) * 14, :] = total[i * 16 : i * 16 + 14, 64:]


def body(acts, grads, basis_in, basis_out, doc_lengths):
    x, zh, core = lax.axis_index("x"), lax.axis_index("zh"), lax.axis_index("core")
    place = jnp.stack([x, zh, core]).astype(jnp.int32)
    tok, fin = acts.shape
    fout = grads.shape[1]
    rows = basis_in.shape[0] // NX
    tokens = NX * tok

    packed, payload = call(
        pack,
        (in_hbm((CHIPS, 16, NC * fin + fout)), jax.ShapeDtypeStruct((fin + fout, tok), BF16)),
        [
            pltpu.VMEM((PARTS, 4 * rows, CHIPS // PARTS * NC * fin), BF16),
            pltpu.VMEM((8, CHIPS * NC * fout), BF16),
            pltpu.VMEM((tok, fout), BF16),
            pltpu.VMEM((fout, tok), BF16),
            pltpu.VMEM((PARTS, CHIPS // PARTS, 16, NC * fin + fout), BF16),
            pltpu.SemaphoreType.DMA((2 * PARTS + 4,)),
        ],
        (place, *map(from_hbm, (basis_in, basis_out, acts.T, grads))),
        1 << 20,
        in_specs=[SMEM] + [ANY] * 4,
        out_spec=ANY,
    )
    packed = lax.all_to_all(packed, ("zl", "y"), split_axis=0, concat_axis=0, tiled=True)

    own = [payload] + [from_offset(payload, "x", NX, s) for s in range(1, NX)]
    other = [from_offset(v, "core", NC, 1) for v in own]

    parts = call(
        project,
        in_hbm((CHIPS, 16, tokens + 128)),
        [
            pltpu.VMEM((2 * CHIPS * 16, 128), F32),
            pltpu.VMEM((CHIPS * 16, 128), F32),
            *[pltpu.VMEM((CHIPS, 16, 256), BF16)] * NX,
            pltpu.VMEM((CHIPS, 16, 128), BF16),
            pltpu.SemaphoreType.DMA((5,)),
        ],
        (place, *map(in_vmem, (packed, *own, *other))),
        2 * 512 * 1024 * 1024,
        out_spec=ANY,
    )
    parts = lax.all_to_all(parts, ("zl", "y"), split_axis=0, concat_axis=0, tiled=True)
    lens = jnp.pad(doc_lengths.astype(F32), ((0, 0), (0, 124)))
    proj_in, proj_out = call(
        add_up,
        (jax.ShapeDtypeStruct((16, tokens), BF16), in_hbm((64, 16, 128))),
        [pltpu.VMEM((16, tokens), F32), pltpu.VMEM((16, 128), F32)],
        (place, lens, in_vmem(parts)),
        32 * 16 * 1152,
    )

    proj_out = lax.all_to_all(proj_out, ("zl", "y", "core"), split_axis=0, concat_axis=0, tiled=True)
    proj_in = lax.all_gather(proj_in, "x")
    block = jax.ShapeDtypeStruct((NX * rows, 64), F32)
    send, keep = call(
        documents,
        (block, block),
        [pltpu.VMEM((64 * 16, 128), F32)],
        (place, *map(in_vmem, (proj_out, proj_in))),
        2 * 4 * 256 * 256 * 128,
    )
    both = lax.all_gather(send, "zh")
    return (keep + jnp.where(zh == 0, both[1], both[0])).T


def solution(mesh):
    fine = Mesh(mesh.devices.reshape(NX, NZH, NZL, NY, NC), ("x", "zh", "zl", "y", "core"))
    dp, mp = ("x", "zh"), ("zl", "y", "core")
    in_specs = (P(dp, mp), P(dp, mp), P(mp, None), P(mp, None), P(dp, None))
    return jax.shard_map(body, mesh=fine, in_specs=in_specs, out_specs=P(dp, mp), check_vma=False)
```

```python
import jax
import jax.numpy as jnp
from jax import lax
from jax.experimental import pallas as pl
from jax.experimental.pallas import tpu as pltpu
from jax.sharding import Mesh, PartitionSpec as P

NX, NZH, NZL, NY, NC = 4, 2, 4, 8, 2
CHIPS = NZL * NY
PARTS = 8
BF16, F32 = jnp.bfloat16, jnp.float32
SMEM = pl.BlockSpec(memory_space=pltpu.SMEM)
VMEM = pl.BlockSpec(memory_space=pltpu.VMEM)
ANY = pl.BlockSpec(memory_space=pl.ANY)


def from_offset(value, axis, size, offset):
    return lax.ppermute(value, axis, [((i + offset) % size, i) for i in range(size)])


def call(kernel, shapes, scratch, operands, flops, in_specs=None, out_spec=VMEM):
    size = sum(a.size * a.dtype.itemsize for a in operands)
    return pl.pallas_call(
        kernel,
        out_shape=shapes,
        in_specs=in_specs or [SMEM] + [VMEM] * (len(operands) - 1),
        out_specs=jax.tree.map(lambda _: out_spec, shapes),
        scratch_shapes=scratch,
        compiler_params=pltpu.CompilerParams(vmem_limit_bytes=40 << 20),
        cost_estimate=pl.CostEstimate(flops=flops, bytes_accessed=size, transcendentals=0),
    )(*operands)


def in_vmem(value):
    return pltpu.with_memory_space_constraint(value, pltpu.VMEM)


def from_hbm(value):
    return pltpu.with_memory_space_constraint(value, pltpu.HBM)


def in_hbm(shape):
    return pltpu.HBM(shape, BF16)


def pack(place, basis_ref, out_rows_ref, acts_ref, grads_ref, packed_ref, payload_ref, *scratch):
    basis, out_rows, grads, turned, packed, sems = scratch
    fin, fout = acts_ref.shape[0], grads_ref.shape[1]
    width, chips = NC * fin, CHIPS // PARTS
    loads = [
        pltpu.make_async_copy(out_rows_ref, out_rows, sems.at[0]),
        pltpu.make_async_copy(grads_ref, grads, sems.at[1]),
    ]
    for i in range(PARTS):
        cols = pl.ds(i * chips * width, chips * width)
        loads.append(pltpu.make_async_copy(basis_ref.at[:, cols], basis.at[i], sems.at[2 + i]))
    stores = [pltpu.make_async_copy(acts_ref, payload_ref.at[pl.ds(0, fin)], sems.at[2 + PARTS])]
    for copy in loads + stores:
        copy.start()
    loads[0].wait()
    for c in range(CHIPS):
        out = out_rows[:, c * NC * fout : (c + 1) * NC * fout].astype(F32)
        out = jnp.concatenate([out[:, :fout], out[:, fout:]], axis=0).astype(BF16)
        packed[c // chips, c % chips, :, width:] = out
    loads[1].wait()
    turned[...] = grads[...].astype(F32).T.astype(BF16)
    stores.append(pltpu.make_async_copy(turned, payload_ref.at[pl.ds(fin, fout)], sems.at[3 + PARTS]))
    stores[-1].start()
    for i in range(PARTS):
        loads[2 + i].wait()
        for x in range(NX):

            @pl.when(place[0] == x)
            def _():
                for c in range(chips):
                    rows = basis[i, :, c * width : (c + 1) * width].astype(F32)[x * 14 : (x + 1) * 14]
                    rows = jnp.concatenate([rows, jnp.zeros((2, width), F32)], axis=0)
                    packed[i, c, :, :width] = rows.astype(BF16)

        there = packed_ref.at[pl.ds(i * chips, chips)]
        stores.append(pltpu.make_async_copy(packed.at[i], there, sems.at[4 + PARTS + i]))
        stores[-1].start()
    for store in stores:
        store.wait()


def project(place, packed_ref, *refs):
    own, other, parts_ref = refs[:NX], refs[NX : 2 * NX], refs[2 * NX]
    wide, low, *outs, sems = refs[2 * NX + 1 :]
    x, core = place[0], place[2]
    fout = parts_ref.shape[2] - NX * 256
    fin = own[0].shape[0] - fout
    tokens, height = NX * 256, CHIPS * 16

    def by_core(halves):
        return jnp.where(core == 0, halves[0], halves[1]), jnp.where(core == 0, halves[1], halves[0])

    left = packed_ref[:, :, : NC * fin].reshape(height, NC * fin)
    left = by_core([left[:, c * fin : (c + 1) * fin] for c in range(NC)])
    rows_out = packed_ref[pl.ds(x * 8, 8), :, NC * fin :].astype(F32).reshape(8, NC, 8, fout)
    rows_out = by_core([rows_out[:, c].reshape(64, fout).astype(BF16) for c in range(NC)])
    results, highs = [], []
    for s in range(NX):
        out = 0.0
        for k, pieces in enumerate((own, other)):
            out += jnp.dot(rows_out[k], pieces[s][fin:, :], preferred_element_type=F32)
        highs.append(out)
        rest = out - out.astype(BF16).astype(F32)
        for h in range(2):
            for half in range(2):
                value = rest[half * 32 : half * 32 + 32, h * 128 : (h + 1) * 128]
                low[pl.ds(half * 8 + s * 2 + h, CHIPS, stride=16), :] = value
    outs[NX][...] = low[...].astype(BF16).reshape(CHIPS, 16, 128)
    results.append(pltpu.make_async_copy(outs[NX], parts_ref.at[:, :, pl.ds(tokens, 128)], sems.at[NX]))
    results[-1].start()
    for s in range(NX):
        part = 0.0
        for k, pieces in enumerate((own, other)):
            part += jnp.dot(left[k], pieces[s][:fin, :], preferred_element_type=F32)
        for h in range(2):
            block = slice(h * 128, (h + 1) * 128)
            wide[pl.ds(h * height, height), :] = part[:, block]
            for half in range(2):
                value = highs[s][half * 32 : half * 32 + 32, block]
                wide[pl.ds(h * height + 14 + half, CHIPS, stride=16), :] = value
            outs[s][:, :, block] = wide[h * height : (h + 1) * height].astype(BF16).reshape(CHIPS, 16, 128)
        results.append(pltpu.make_async_copy(outs[s], parts_ref.at[:, :, pl.ds(s * 256, 256)], sems.at[s]))
        results[-1].start()
    for result in results:
        result.wait()


def add_up(place, lens_ref, parts_ref, in_ref, out_ref, wide, narrow, rows_in, spread, sems):
    x = place[0]
    tokens = wide.shape[1]
    total = parts_ref[0].astype(F32)
    for i in range(1, CHIPS):
        total = total + parts_ref[i].astype(F32)
    sources = [lax.rem(x + s, NX) for s in range(NX)]
    for s in range(NX):
        for half in range(2):
            for h in range(2):
                col, row = s * 2 + h, half * 8 + s * 2 + h
                value = total[14 + half : 15 + half, col * 128 : (col + 1) * 128] + total[row : row + 1, tokens:]
                narrow[pl.ds(half * 8 + sources[s] * 2 + h, 1), :] = value
    spread[...] = jnp.broadcast_to(narrow[...].astype(BF16)[None], spread.shape)
    first = pltpu.make_async_copy(spread, out_ref, sems.at[0])
    first.start()
    for s in range(NX):
        there = pl.ds(pl.multiple_of(sources[s] * 256, 256), 256)
        wide[:, there] = total[:, s * 256 : (s + 1) * 256]
    wide[14:15, :128] = lens_ref[...]
    rows_in[...] = wide[...].astype(BF16)
    second = pltpu.make_async_copy(rows_in, in_ref, sems.at[1])
    second.start()
    first.wait()
    second.wait()


def documents(place, out_ref, in_ref, send_ref, keep_ref, rows_out):
    zh = place[1]
    rows_out[...] = out_ref[...].astype(F32).reshape(64 * 16, 128)
    position = lax.broadcasted_iota(jnp.int32, (1, 256), 1).astype(F32)
    total = jnp.zeros((NX * 16, 128), F32)
    for g in range(NX):
        left = in_ref[:, :, g * 256 : (g + 1) * 256].astype(F32).reshape(NX * 16, 256)
        lens = in_ref[g, :, :128].astype(F32)[14:15, :4]
        right = []
        for h in range(2):
            cut = [
                rows_out[pl.ds((zl * 16 + core) * 16 + block * 8 + g * 2 + h, NY, stride=32), :]
                for block in (1 - zh, zh)
                for zl in range(NZL)
                for core in range(NC)
            ]
            right.append(jnp.concatenate(cut, axis=0))
        right = jnp.concatenate(right, axis=1).astype(BF16)
        masked, start = [], jnp.zeros((1, 1), F32)
        for d in range(4):
            end = start + lens[:, d : d + 1]
            inside = (position >= start) & (position < end)
            masked.append(jnp.where(inside, left, 0.0).astype(BF16))
            start = end
        product = lax.dot_general(
            jnp.concatenate(masked, axis=0), right, (((1,), (1,)), ((), ())), preferred_element_type=F32
        )
        for d in range(4):
            one = product[d * 64 : (d + 1) * 64]
            total = total + one * one
    total = total * (1.0 / 2048.0)
    for i in range(NX):
        send_ref[i * 14 : (i + 1) * 14, :] = total[i * 16 : i * 16 + 14, :64]
        keep_ref[i * 14 : (i + 1) * 14, :] = total[i * 16 : i * 16 + 14, 64:]


def body(acts, grads, basis_in, basis_out, doc_lengths):
    x, zh, core = lax.axis_index("x"), lax.axis_index("zh"), lax.axis_index("core")
    place = jnp.stack([x, zh, core]).astype(jnp.int32)
    tok, fin = acts.shape
    fout = grads.shape[1]
    rows = basis_in.shape[0] // NX
    tokens = NX * tok

    packed, payload = call(
        pack,
        (in_hbm((CHIPS, 16, NC * fin + fout)), jax.ShapeDtypeStruct((fin + fout, tok), BF16)),
        [
            pltpu.VMEM((PARTS, 4 * rows, CHIPS // PARTS * NC * fin), BF16),
            pltpu.VMEM((8, CHIPS * NC * fout), BF16),
            pltpu.VMEM((tok, fout), BF16),
            pltpu.VMEM((fout, tok), BF16),
            pltpu.VMEM((PARTS, CHIPS // PARTS, 16, NC * fin + fout), BF16),
            pltpu.SemaphoreType.DMA((2 * PARTS + 4,)),
        ],
        (place, *map(from_hbm, (basis_in, basis_out, acts.T, grads))),
        1 << 20,
        in_specs=[SMEM] + [ANY] * 4,
        out_spec=ANY,
    )
    packed = lax.all_to_all(packed, ("zl", "y"), split_axis=0, concat_axis=0, tiled=True)

    own = [payload] + [from_offset(payload, "x", NX, s) for s in range(1, NX)]
    other = [from_offset(v, "core", NC, 1) for v in own]

    parts = call(
        project,
        in_hbm((CHIPS, 16, tokens + 128)),
        [
            pltpu.VMEM((2 * CHIPS * 16, 128), F32),
            pltpu.VMEM((CHIPS * 16, 128), F32),
            *[pltpu.VMEM((CHIPS, 16, 256), BF16)] * NX,
            pltpu.VMEM((CHIPS, 16, 128), BF16),
            pltpu.SemaphoreType.DMA((5,)),
        ],
        (place, *map(in_vmem, (packed, *own, *other))),
        2 * 512 * 1024 * 1024,
        out_spec=ANY,
    )
    parts = lax.all_to_all(parts, ("zl", "y"), split_axis=0, concat_axis=0, tiled=True)
    lens = jnp.pad(doc_lengths.astype(F32), ((0, 0), (0, 124)))
    proj_in, proj_out = call(
        add_up,
        (jax.ShapeDtypeStruct((16, tokens), BF16), in_hbm((64, 16, 128))),
        [
            pltpu.VMEM((16, tokens), F32),
            pltpu.VMEM((16, 128), F32),
            pltpu.VMEM((16, tokens), BF16),
            pltpu.VMEM((64, 16, 128), BF16),
            pltpu.SemaphoreType.DMA((2,)),
        ],
        (place, lens, in_vmem(parts)),
        32 * 16 * 1152,
        out_spec=ANY,
    )

    proj_out = lax.all_to_all(proj_out, ("zl", "y", "core"), split_axis=0, concat_axis=0, tiled=True)
    proj_in = lax.all_gather(proj_in, "x")
    block = jax.ShapeDtypeStruct((NX * rows, 64), F32)
    send, keep = call(
        documents,
        (block, block),
        [pltpu.VMEM((64 * 16, 128), F32)],
        (place, *map(in_vmem, (proj_out, proj_in))),
        2 * 4 * 256 * 256 * 128,
    )
    both = lax.all_gather(send, "zh")
    return (keep + jnp.where(zh == 0, both[1], both[0])).T


def solution(mesh):
    fine = Mesh(mesh.devices.reshape(NX, NZH, NZL, NY, NC), ("x", "zh", "zl", "y", "core"))
    dp, mp = ("x", "zh"), ("zl", "y", "core")
    in_specs = (P(dp, mp), P(dp, mp), P(mp, None), P(mp, None), P(dp, None))
    return jax.shard_map(body, mesh=fine, in_specs=in_specs, out_specs=P(dp, mp), check_vma=False)
```

```python
import jax
import jax.numpy as jnp
from jax import lax
from jax.experimental import pallas as pl
from jax.experimental.pallas import tpu as pltpu
from jax.sharding import Mesh, PartitionSpec as P

NX, NZH, NZL, NY, NC = 4, 2, 4, 8, 2
CHIPS = NZL * NY
PARTS = 16
BF16, F32 = jnp.bfloat16, jnp.float32
SMEM = pl.BlockSpec(memory_space=pltpu.SMEM)
VMEM = pl.BlockSpec(memory_space=pltpu.VMEM)
ANY = pl.BlockSpec(memory_space=pl.ANY)


def from_offset(value, axis, size, offset):
    return lax.ppermute(value, axis, [((i + offset) % size, i) for i in range(size)])


def call(kernel, shapes, scratch, operands, flops, in_specs=None, out_spec=VMEM):
    size = sum(a.size * a.dtype.itemsize for a in operands)
    return pl.pallas_call(
        kernel,
        out_shape=shapes,
        in_specs=in_specs or [SMEM] + [VMEM] * (len(operands) - 1),
        out_specs=jax.tree.map(lambda _: out_spec, shapes),
        scratch_shapes=scratch,
        compiler_params=pltpu.CompilerParams(vmem_limit_bytes=40 << 20),
        cost_estimate=pl.CostEstimate(flops=flops, bytes_accessed=size, transcendentals=0),
    )(*operands)


def in_vmem(value):
    return pltpu.with_memory_space_constraint(value, pltpu.VMEM)


def from_hbm(value):
    return pltpu.with_memory_space_constraint(value, pltpu.HBM)


def in_hbm(shape):
    return pltpu.HBM(shape, BF16)


def pack(place, basis_ref, out_rows_ref, acts_ref, grads_ref, packed_ref, payload_ref, *scratch):
    basis, out_rows, grads, turned, packed, sems = scratch
    fin, fout = acts_ref.shape[0], grads_ref.shape[1]
    width, chips = NC * fin, CHIPS // PARTS
    loads = [
        pltpu.make_async_copy(out_rows_ref, out_rows, sems.at[0]),
        pltpu.make_async_copy(grads_ref, grads, sems.at[1]),
    ]
    for i in range(PARTS):
        cols = pl.ds(i * chips * width, chips * width)
        loads.append(pltpu.make_async_copy(basis_ref.at[:, cols], basis.at[i], sems.at[2 + i]))
    stores = [pltpu.make_async_copy(acts_ref, payload_ref.at[pl.ds(0, fin)], sems.at[2 + PARTS])]
    for copy in loads + stores:
        copy.start()
    loads[0].wait()
    for c in range(CHIPS):
        out = out_rows[:, c * NC * fout : (c + 1) * NC * fout].astype(F32)
        out = jnp.concatenate([out[:, :fout], out[:, fout:]], axis=0).astype(BF16)
        packed[c // chips, c % chips, :, width:] = out
    loads[1].wait()
    turned[...] = grads[...].astype(F32).T.astype(BF16)
    stores.append(pltpu.make_async_copy(turned, payload_ref.at[pl.ds(fin, fout)], sems.at[3 + PARTS]))
    stores[-1].start()
    for i in range(PARTS):
        loads[2 + i].wait()
        for x in range(NX):

            @pl.when(place[0] == x)
            def _():
                for c in range(chips):
                    rows = basis[i, :, c * width : (c + 1) * width].astype(F32)[x * 14 : (x + 1) * 14]
                    rows = jnp.concatenate([rows, jnp.zeros((2, width), F32)], axis=0)
                    packed[i, c, :, :width] = rows.astype(BF16)

        there = packed_ref.at[pl.ds(i * chips, chips)]
        stores.append(pltpu.make_async_copy(packed.at[i], there, sems.at[4 + PARTS + i]))
        stores[-1].start()
    for store in stores:
        store.wait()


def project(place, packed_ref, *refs):
    own, other, parts_ref = refs[:NX], refs[NX : 2 * NX], refs[2 * NX]
    wide, low, *outs, sems = refs[2 * NX + 1 :]
    x, core = place[0], place[2]
    fout = parts_ref.shape[2] - NX * 256
    fin = own[0].shape[0] - fout
    tokens, height = NX * 256, CHIPS * 16

    def by_core(halves):
        return jnp.where(core == 0, halves[0], halves[1]), jnp.where(core == 0, halves[1], halves[0])

    left = packed_ref[:, :, : NC * fin].reshape(height, NC * fin)
    left = by_core([left[:, c * fin : (c + 1) * fin] for c in range(NC)])
    rows_out = packed_ref[pl.ds(x * 8, 8), :, NC * fin :].astype(F32).reshape(8, NC, 8, fout)
    rows_out = by_core([rows_out[:, c].reshape(64, fout).astype(BF16) for c in range(NC)])
    results = []
    for s in range(NX):
        part, out = 0.0, 0.0
        for k, pieces in enumerate((own, other)):
            part += jnp.dot(left[k], pieces[s][:fin, :], preferred_element_type=F32)
            out += jnp.dot(rows_out[k], pieces[s][fin:, :], preferred_element_type=F32)
        rest = out - out.astype(BF16).astype(F32)
        for h in range(2):
            block = slice(h * 128, (h + 1) * 128)
            wide[pl.ds(h * height, height), :] = part[:, block]
            for half in range(2):
                wide[pl.ds(h * height + 14 + half, CHIPS, stride=16), :] = out[half * 32 : half * 32 + 32, block]
                low[pl.ds(half * 8 + s * 2 + h, CHIPS, stride=16), :] = rest[half * 32 : half * 32 + 32, block]
            outs[s][:, :, block] = wide[h * height : (h + 1) * height].astype(BF16).reshape(CHIPS, 16, 128)
        results.append(pltpu.make_async_copy(outs[s], parts_ref.at[:, :, pl.ds(s * 256, 256)], sems.at[s]))
        results[-1].start()
    outs[NX][...] = low[...].astype(BF16).reshape(CHIPS, 16, 128)
    results.append(pltpu.make_async_copy(outs[NX], parts_ref.at[:, :, pl.ds(tokens, 128)], sems.at[NX]))
    results[-1].start()
    for result in results:
        result.wait()


def add_up(place, lens_ref, parts_ref, in_ref, out_ref, wide, narrow):
    x = place[0]
    tokens = wide.shape[1]
    total = parts_ref[0].astype(F32)
    for i in range(1, CHIPS):
        total = total + parts_ref[i].astype(F32)
    for s in range(NX):
        source = lax.rem(x + s, NX)
        wide[:, pl.ds(pl.multiple_of(source * 256, 256), 256)] = total[:, s * 256 : (s + 1) * 256]
        for half in range(2):
            for h in range(2):
                col, row = s * 2 + h, half * 8 + s * 2 + h
                value = total[14 + half : 15 + half, col * 128 : (col + 1) * 128] + total[row : row + 1, tokens:]
                narrow[pl.ds(half * 8 + source * 2 + h, 1), :] = value
    wide[14:15, :128] = lens_ref[...]
    in_ref[...] = wide[...].astype(BF16)
    out_ref[...] = jnp.broadcast_to(narrow[...].astype(BF16)[None], out_ref.shape)


def documents(place, out_ref, in_ref, send_ref, keep_ref, rows_out):
    zh = place[1]
    rows_out[...] = out_ref[...].astype(F32).reshape(64 * 16, 128)
    position = lax.broadcasted_iota(jnp.int32, (1, 256), 1).astype(F32)
    total = jnp.zeros((NX * 16, 128), F32)
    for g in range(NX):
        left = in_ref[:, :, g * 256 : (g + 1) * 256].astype(F32).reshape(NX * 16, 256)
        lens = in_ref[g, :, :128].astype(F32)[14:15, :4]
        right = []
        for h in range(2):
            cut = [
                rows_out[pl.ds((zl * 16 + core) * 16 + block * 8 + g * 2 + h, NY, stride=32), :]
                for block in (1 - zh, zh)
                for zl in range(NZL)
                for core in range(NC)
            ]
            right.append(jnp.concatenate(cut, axis=0))
        right = jnp.concatenate(right, axis=1).astype(BF16)
        masked, start = [], jnp.zeros((1, 1), F32)
        for d in range(4):
            end = start + lens[:, d : d + 1]
            inside = (position >= start) & (position < end)
            masked.append(jnp.where(inside, left, 0.0).astype(BF16))
            start = end
        product = lax.dot_general(
            jnp.concatenate(masked, axis=0), right, (((1,), (1,)), ((), ())), preferred_element_type=F32
        )
        for d in range(4):
            one = product[d * 64 : (d + 1) * 64]
            total = total + one * one
    total = total * (1.0 / 2048.0)
    for i in range(NX):
        send_ref[i * 14 : (i + 1) * 14, :] = total[i * 16 : i * 16 + 14, :64]
        keep_ref[i * 14 : (i + 1) * 14, :] = total[i * 16 : i * 16 + 14, 64:]


def body(acts, grads, basis_in, basis_out, doc_lengths):
    x, zh, core = lax.axis_index("x"), lax.axis_index("zh"), lax.axis_index("core")
    place = jnp.stack([x, zh, core]).astype(jnp.int32)
    tok, fin = acts.shape
    fout = grads.shape[1]
    rows = basis_in.shape[0] // NX
    tokens = NX * tok

    packed, payload = call(
        pack,
        (in_hbm((CHIPS, 16, NC * fin + fout)), jax.ShapeDtypeStruct((fin + fout, tok), BF16)),
        [
            pltpu.VMEM((PARTS, 4 * rows, CHIPS // PARTS * NC * fin), BF16),
            pltpu.VMEM((8, CHIPS * NC * fout), BF16),
            pltpu.VMEM((tok, fout), BF16),
            pltpu.VMEM((fout, tok), BF16),
            pltpu.VMEM((PARTS, CHIPS // PARTS, 16, NC * fin + fout), BF16),
            pltpu.SemaphoreType.DMA((2 * PARTS + 4,)),
        ],
        (place, *map(from_hbm, (basis_in, basis_out, acts.T, grads))),
        1 << 20,
        in_specs=[SMEM] + [ANY] * 4,
        out_spec=ANY,
    )
    packed = lax.all_to_all(packed, ("zl", "y"), split_axis=0, concat_axis=0, tiled=True)

    own = [payload] + [from_offset(payload, "x", NX, s) for s in range(1, NX)]
    other = [from_offset(v, "core", NC, 1) for v in own]

    parts = call(
        project,
        in_hbm((CHIPS, 16, tokens + 128)),
        [
            pltpu.VMEM((2 * CHIPS * 16, 128), F32),
            pltpu.VMEM((CHIPS * 16, 128), F32),
            *[pltpu.VMEM((CHIPS, 16, 256), BF16)] * NX,
            pltpu.VMEM((CHIPS, 16, 128), BF16),
            pltpu.SemaphoreType.DMA((5,)),
        ],
        (place, *map(in_vmem, (packed, *own, *other))),
        2 * 512 * 1024 * 1024,
        out_spec=ANY,
    )
    parts = lax.all_to_all(parts, ("zl", "y"), split_axis=0, concat_axis=0, tiled=True)
    lens = jnp.pad(doc_lengths.astype(F32), ((0, 0), (0, 124)))
    proj_in, proj_out = call(
        add_up,
        (jax.ShapeDtypeStruct((16, tokens), BF16), in_hbm((64, 16, 128))),
        [pltpu.VMEM((16, tokens), F32), pltpu.VMEM((16, 128), F32)],
        (place, lens, in_vmem(parts)),
        32 * 16 * 1152,
    )

    proj_out = lax.all_to_all(proj_out, ("zl", "y", "core"), split_axis=0, concat_axis=0, tiled=True)
    proj_in = lax.all_gather(proj_in, "x")
    block = jax.ShapeDtypeStruct((NX * rows, 64), F32)
    send, keep = call(
        documents,
        (block, block),
        [pltpu.VMEM((64 * 16, 128), F32)],
        (place, *map(in_vmem, (proj_out, proj_in))),
        2 * 4 * 256 * 256 * 128,
    )
    both = lax.all_gather(send, "zh")
    return (keep + jnp.where(zh == 0, both[1], both[0])).T


def solution(mesh):
    fine = Mesh(mesh.devices.reshape(NX, NZH, NZL, NY, NC), ("x", "zh", "zl", "y", "core"))
    dp, mp = ("x", "zh"), ("zl", "y", "core")
    in_specs = (P(dp, mp), P(dp, mp), P(mp, None), P(mp, None), P(dp, None))
    return jax.shard_map(body, mesh=fine, in_specs=in_specs, out_specs=P(dp, mp), check_vma=False)
```
